32 devices in a mesh: section: 2 (over core), dp: 16 (over z, y, x).
Axes of the slice: x: 2, y: 2, z: 4, core: 2. Of those that a mesh axis runs over, the one named last changes fastest.
Arguments:
- features: bfloat16 [3, 32, 2048, 652], P(None, 'dp'), may hold values from -24 to 24
- lengths: int32 [3, 32], P(None, 'dp'), may hold values from 512 to 2048, as said below
- gain_first: float32 [652], replicated, may hold values from 0.5 to 1.5
- shift_first: float32 [652], replicated, may hold values from -3 to 3
- conv_first: bfloat16 [5, 652, 768], replicated, may hold values from -0.109375 to 0.109375
- bias_first: float32 [768], replicated, may hold values from -3 to 3
- gain_second: float32 [768], replicated, may hold values from 0.5 to 1.5
- shift_second: float32 [768], replicated, may hold values from -3 to 3
- conv_second: bfloat16 [3, 768, 384], replicated, may hold values from -0.125 to 0.125
- gain_third: float32 [384], replicated, may hold values from 0.5 to 1.5
- shift_third: float32 [384], replicated, may hold values from -3 to 3
- conv_point: bfloat16 [384, 768], replicated, may hold values from -0.3125 to 0.3125
- bias_point: float32 [768], replicated, may hold values from -3 to 3
- mean_first: float32 [652], replicated, may hold values from -4 to 4
- variance_first: float32 [652], replicated, may hold values from 0.5 to 2
- mean_second: float32 [768], replicated, may hold values from -4 to 4
- variance_second: float32 [768], replicated, may hold values from 0.5 to 2
- mean_third: float32 [384], replicated, may hold values from -4 to 4
- variance_third: float32 [384], replicated, may hold values from 0.5 to 2
- cotangent: bfloat16 [3, 32, 1024, 768], P(None, 'dp'), may hold values from -6 to 6
Outputs:
- block_output: bfloat16 [3, 32, 1024, 768], P(None, 'dp', None, 'section')
- input_grad: bfloat16 [3, 32, 2048, 652], P(None, 'dp', None, 'section')
- grad_gain_first: float32 [652], replicated
- grad_shift_first: float32 [652], replicated
- grad_conv_first: float32 [5, 652, 768], replicated
- grad_bias_first: float32 [768], replicated
- grad_gain_second: float32 [768], replicated
- grad_shift_second: float32 [768], replicated
- grad_conv_second: float32 [3, 768, 384], replicated
- grad_gain_third: float32 [384], replicated
- grad_shift_third: float32 [384], replicated
- grad_point: float32 [384, 768], replicated
- grad_bias_point: float32 [768], replicated
- new_mean_first: float32 [652], replicated
- new_variance_first: float32 [652], replicated
- new_mean_second: float32 [768], replicated
- new_variance_second: float32 [768], replicated
- new_mean_third: float32 [384], replicated
- new_variance_third: float32 [384], replicated
The draws below stay inside these ranges and needn't reach their ends.
Inputs may be any that keep to these rules, and one draw needn't show every extreme that they name: `lengths`: in every micro-batch some window has all 2048 bins valid.
All inputs are finite; a program needn't handle non-finite values.
Results may differ from the reference program's by a relative error of at most 0.008.
The reference program's roundings to bfloat16 on the way count: a program that leaves them out, or rounds other values in their place, can miss the bound.
Values may be sent and summed in bfloat16 or wider, within the bound.
No kernel may reach another device: no remote copies, remote signals or barrier semaphores. Data moves between devices by JAX's collectives and lax.ppermute only.
A program may use at most 576 MiB of HBM per device.

```python
import math
import jax
import jax.numpy as jnp
from jax import lax

C_IN = 652
C_MID = 768
C_RES = 384
KERNEL_A = 5
KERNEL_B = 3
BINS = 2048
MICRO = 3
POOLED = 1024
WINDOWS = 32


def draw_features(key, part):
    key = jax.random.fold_in(key, 11)
    full_shape = (MICRO, WINDOWS, BINS, C_IN)
    window_pos = jnp.arange(WINDOWS, dtype=jnp.float32) / max(WINDOWS - 1, 1)
    window_scale = 3.0 ** window_pos
    values = jnp.clip(jax.random.normal(key, full_shape, jnp.float32), -6.0, 6.0) * window_scale[None, :, None, None]
    return values.astype(jnp.bfloat16)


def draw_lengths(key, part):
    key = jax.random.fold_in(key, 23)
    drawn_lengths = jax.random.randint(key, (MICRO, WINDOWS), BINS // 4, BINS + 1, dtype=jnp.int32)
    longest = jax.random.randint(jax.random.fold_in(key, 2), (MICRO, 1), 0, WINDOWS, dtype=jnp.int32)
    columns = jnp.arange(WINDOWS, dtype=jnp.int32)[None, :]
    return jnp.where(columns == longest, BINS, drawn_lengths).astype(jnp.int32)


def levels(stream_key, shape, pieces, least, high):
    loudness, own = 1.0, jax.random.fold_in(stream_key, 6)
    for dim, blocks in pieces:
        draws = jnp.exp(jax.random.uniform(jax.random.fold_in(own, dim), (blocks,), jnp.float32, least / len(pieces), high / len(pieces)))
        loudness = loudness * jnp.repeat(draws, shape[dim] // blocks).reshape([-1 if axis == dim else 1 for axis in range(len(shape))])
    return loudness


def scatter_about(own_key, shape, spread, reach, pieces=(), kind=jnp.bfloat16):
    drawn = spread * jax.random.normal(own_key, shape, jnp.float32)
    if pieces:
        drawn = drawn * levels(own_key, shape, pieces, -0.22, 0.18)
    return jnp.clip(drawn, -reach, reach).astype(kind)


def setup_inputs(seed: int = 0) -> dict:
    arg_keys = jax.random.split(jax.random.key(seed), 21)
    return {
        "features": draw_features(jax.random.fold_in(arg_keys[20], 71), 0),
        "lengths": draw_lengths(jax.random.fold_in(arg_keys[20], 71), 0),
        "gain_first": jnp.clip(jax.random.uniform(arg_keys[2], (C_IN,), jnp.float32, 0.5, 1.5), 0.5, 1.5),
        "shift_first": scatter_about(arg_keys[3], (C_IN,), 0.5, 3.0, (), jnp.float32),
        "conv_first": scatter_about(arg_keys[4], (KERNEL_A, C_IN, C_MID), (KERNEL_A * C_IN) ** -0.5, 0.109375),
        "bias_first": scatter_about(arg_keys[5], (C_MID,), 0.5, 3.0, (), jnp.float32),
        "gain_second": jnp.clip(jax.random.uniform(arg_keys[6], (C_MID,), jnp.float32, 0.5, 1.5), 0.5, 1.5),
        "shift_second": scatter_about(arg_keys[7], (C_MID,), 0.5, 3.0, (), jnp.float32),
        "conv_second": scatter_about(arg_keys[8], (KERNEL_B, C_MID, C_RES), (KERNEL_B * C_MID) ** -0.5, 0.125),
        "gain_third": jnp.clip(jax.random.uniform(arg_keys[9], (C_RES,), jnp.float32, 0.5, 1.5), 0.5, 1.5),
        "shift_third": scatter_about(arg_keys[10], (C_RES,), 0.5, 3.0, (), jnp.float32),
        "conv_point": scatter_about(arg_keys[11], (C_RES, C_MID), C_RES ** -0.5, 0.3125),
        "bias_point": scatter_about(arg_keys[12], (C_MID,), 0.5, 3.0, (), jnp.float32),
        "mean_first": scatter_about(arg_keys[13], (C_IN,), 1.0, 4.0, (), jnp.float32),
        "variance_first": jnp.clip(jnp.exp(jax.random.uniform(arg_keys[14], (C_IN,), jnp.float32, math.log(0.5), math.log(2.0))), 0.5, 2.0),
        "mean_second": scatter_about(arg_keys[15], (C_MID,), 1.0, 4.0, (), jnp.float32),
        "variance_second": jnp.clip(jnp.exp(jax.random.uniform(arg_keys[16], (C_MID,), jnp.float32, math.log(0.5), math.log(2.0))), 0.5, 2.0),
        "mean_third": scatter_about(arg_keys[17], (C_RES,), 1.0, 4.0, (), jnp.float32),
        "variance_third": jnp.clip(jnp.exp(jax.random.uniform(arg_keys[18], (C_RES,), jnp.float32, math.log(0.5), math.log(2.0))), 0.5, 2.0),
        "cotangent": scatter_about(arg_keys[19], (MICRO, WINDOWS, POOLED, C_MID), 1.0, 6.0, ((1, 16),)),
    }


EPSILON = 1e-05
MOMENTUM = 0.4

@jax.custom_vjp
def low(v):
    return lax.optimization_barrier(v.astype(jnp.bfloat16)).astype(jnp.float32)

@jax.custom_vjp
def low_back(v):
    return v

def low_keep(v):
    return (low(v), None)

def low_pass(kept, grad):
    return (grad,)

def back_keep(v):
    return (v, None)

def back_low(kept, grad):
    return (low(grad),)
low.defvjp(low_keep, low_pass)
low_back.defvjp(back_keep, back_low)

def conv_apply(values, weight):
    kernel_width = weight.shape[0]
    half_width = kernel_width // 2
    length_bins = values.shape[1]
    padded = jnp.pad(values, ((0, 0), (half_width, half_width), (0, 0)))
    result = jnp.zeros(values.shape[:2] + (weight.shape[2],), jnp.float32)
    for offset in range(kernel_width):
        result = result + jnp.einsum('wlc,cd->wld', padded[:, offset:offset + length_bins], weight[offset], precision=lax.Precision.HIGHEST)
    return result

def masked_norm(values, bin_mask, gain, shift):
    valid_count = jnp.sum(bin_mask)
    centre = lax.optimization_barrier(jnp.sum(values * bin_mask, axis=(0, 1))) / valid_count
    variance = lax.optimization_barrier(jnp.sum(values * values * bin_mask, axis=(0, 1))) / valid_count - centre * centre
    normed = bin_mask * ((values - centre) * lax.rsqrt(variance + EPSILON) * gain + shift)
    return (normed, centre, variance)

def forward_batch(params, feats_batch, length_batch):
    gain_first, shift_first, conv_first, bias_first, gain_second, shift_second, conv_second, gain_third, shift_third, conv_point, bias_point = params
    mask_input = (jnp.arange(BINS, dtype=jnp.int32)[None, :] < length_batch[:, None]).astype(jnp.float32)[..., None]
    mask_pooled = (2 * jnp.arange(BINS // 2, dtype=jnp.int32)[None, :] < length_batch[:, None]).astype(jnp.float32)[..., None]
    inputs = feats_batch * mask_input
    normed, centre_a, variance_a = masked_norm(inputs, mask_input, gain_first, shift_first)
    active = low(jax.nn.gelu(normed))
    conv_out = low_back(conv_apply(active, conv_first) + bias_first)
    paired = conv_out.reshape(conv_out.shape[0], BINS // 2, 2, conv_out.shape[2])
    hidden = low_back(low(jnp.logaddexp(paired[:, :, 0], paired[:, :, 1]) * mask_pooled))
    normed, centre_b, variance_b = masked_norm(hidden, mask_pooled, gain_second, shift_second)
    active = low(jax.nn.gelu(normed))
    conv_mid = low_back(conv_apply(active, conv_second))
    normed, centre_c, variance_c = masked_norm(conv_mid, mask_pooled, gain_third, shift_third)
    active = low(jax.nn.gelu(normed))
    branch = jnp.einsum('wlc,cd->wld', active, conv_point, precision=lax.Precision.HIGHEST) + bias_point
    return ((hidden + branch) * mask_pooled, (centre_a, variance_a, centre_b, variance_b, centre_c, variance_c))

def running_update(start_value, history):
    value_now = start_value
    for step_number in range(MICRO):
        value_now = (1.0 - MOMENTUM) * value_now + MOMENTUM * history[step_number]
    return value_now

def reference(features, lengths, gain_first, shift_first, conv_first, bias_first, gain_second, shift_second, conv_second, gain_third, shift_third, conv_point, bias_point, mean_first, variance_first, mean_second, variance_second, mean_third, variance_third, cotangent):
    params = tuple((parameter.astype(jnp.float32) for parameter in (gain_first, shift_first, conv_first, bias_first, gain_second, shift_second, conv_second, gain_third, shift_third, conv_point, bias_point)))

    def stack_forward(weights, feats_all):

        def one_step(carry, items):
            output, stats = forward_batch(weights, items[0], items[1])
            return (carry, (output, stats))
        carry_out, results = lax.scan(jax.checkpoint(one_step), jnp.zeros((), jnp.float32), (feats_all, lengths))
        return (results[0], results[1])
    outputs, pullback, stats = jax.vjp(stack_forward, params, features.astype(jnp.float32), has_aux=True)
    grad_params, grad_features = pullback(cotangent.astype(jnp.float32))
    return (outputs.astype(jnp.bfloat16), grad_features.astype(jnp.bfloat16), grad_params[0], grad_params[1], grad_params[2], grad_params[3], grad_params[4], grad_params[5], grad_params[6], grad_params[7], grad_params[8], grad_params[9], grad_params[10], running_update(mean_first, stats[0]), running_update(variance_first, stats[1]), running_update(mean_second, stats[2]), running_update(variance_second, stats[3]), running_update(mean_third, stats[4]), running_update(variance_third, stats[5]))
```

```python
from math import pi, sqrt

import jax
import jax.numpy as jnp
from jax import lax
from jax.experimental import pallas as pl
from jax.experimental.pallas import tpu as pltpu
from jax.sharding import PartitionSpec as P

EPSILON = 1e-05
MOMENTUM = 0.4
CURVE = sqrt(2.0 / pi)
CUBIC = CURVE * 0.044715
BF16 = jnp.bfloat16
F32 = jnp.float32
LANES = 128
TILE = 256
BOTH = ("section", "dp")


def up(value, step):
    return -(-value // step) * step


def nn(left, right):
    return jnp.dot(left, right, preferred_element_type=F32)


def nt(left, right):
    return lax.dot_general(left, right, (((1,), (1,)), ((), ())), preferred_element_type=F32)


def iota(shape, axis):
    return lax.broadcasted_iota(jnp.int32, shape, axis)


def choose(flag):
    return jnp.where(flag, 1.0, 0.0)


def identity():
    return choose(iota((TILE, TILE), 0) == iota((TILE, TILE), 1)).astype(BF16)


def gelu(v):
    half = 0.5 * v
    return half + half * jnp.tanh(v * (CURVE + CUBIC * (v * v)))


def gelu_slope(v):
    square = v * v
    bent = jnp.tanh(v * (CURVE + CUBIC * square))
    half = 0.5 * v
    slope = (0.5 + 0.5 * bent) + half * (1.0 - bent * bent) * (CURVE + (3.0 * CUBIC) * square)
    return half + half * bent, slope


def column(row):
    return jnp.transpose(jnp.broadcast_to(row, (LANES, row.shape[1])))


def as_row(partial_sums):
    return jnp.sum(jnp.transpose(partial_sums), axis=0, keepdims=True)


def wide(block, lanes):
    return jnp.concatenate([block] * (lanes // LANES), axis=1)


def fold(block):
    parts = [block[:, at : at + LANES] for at in range(0, block.shape[1], LANES)]
    while len(parts) > 1:
        parts = [a + b for a, b in zip(parts[::2], parts[1::2])]
    return parts[0]


def before(block):
    rolled = pltpu.roll(block, 1, 1)
    inner = choose(iota((block.shape[0], LANES), 1) > 0).astype(block.dtype)
    return jnp.concatenate([rolled[:, :LANES] * inner, rolled[:, LANES:]], axis=1)


def after(block):
    last = block.shape[1] - LANES
    rolled = pltpu.roll(block, block.shape[1] - 1, 1)
    inner = choose(iota((block.shape[0], LANES), 1) < LANES - 1).astype(block.dtype)
    return jnp.concatenate([rolled[:, :last], rolled[:, last:] * inner], axis=1)


def aligned(value):
    return value if isinstance(value, int) else pl.multiple_of(value, 16)


def each_rows(total, body, unroll, step=16):
    group = step * unroll
    full = total // group

    def run(index, carry):
        for turn in range(unroll):
            start = pl.multiple_of(index * group + turn * step, step)
            body(pl.ds(start, step), start)
        return carry

    lax.fori_loop(0, full, run, 0)
    for start in range(full * group, total, step):
        body(pl.ds(start, step), start)


def pool_mask(length, lanes, start=0):
    return choose(2 * (iota((1, lanes), 1) + start) < length)


def odd_mask(length, lanes, start=0):
    return choose(2 * (iota((1, lanes), 1) + start) + 1 < length)


def whole(shape, buffered=None):
    zeros = (0,) * len(shape)
    if buffered is None:
        return pl.BlockSpec(shape, lambda *_: zeros)
    return pl.BlockSpec(shape, lambda *_: zeros, pipeline_mode=pl.Buffered(buffered))


def per_batch(shape):
    return pl.BlockSpec((1,) + shape, lambda k, *_: (k,) + (0,) * len(shape))


def per_lanes(shape):
    return pl.BlockSpec((1,) + shape, lambda k, j, _: (k,) + (0,) * (len(shape) - 1) + (j,))


def shape_of(shape, dtype=F32):
    return jax.ShapeDtypeStruct(shape, dtype)


def call(name, body, grid, in_specs, out_specs, out_shape, scratch=(), limit=58):
    return pl.pallas_call(
        body,
        grid_spec=pltpu.PrefetchScalarGridSpec(
            num_scalar_prefetch=1,
            grid=grid,
            in_specs=in_specs,
            out_specs=out_specs,
            scratch_shapes=list(scratch),
        ),
        out_shape=out_shape,
        compiler_params=pltpu.CompilerParams(vmem_limit_bytes=limit * 2**20),
        name=name,
    )


def row_pair(ref, k):
    table = ref[...]
    at = iota(table.shape, 0) - 2 * k
    rows = [jnp.sum(jnp.where(at == r, table, 0.0), axis=0, keepdims=True) for r in range(2)]
    return jnp.concatenate(rows, axis=0)


def put_rows(ref, k, first, second):
    table = ref[...]
    at = iota(table.shape, 0) - 2 * k
    ref[...] = jnp.where(at == 0, first, jnp.where(at == 1, second, table))


def finish_rows(total, count):
    centre = total[0:1] / count
    variance = total[1:2] / count - centre * centre
    return centre, variance, lax.rsqrt(variance + EPSILON)


def first_rows(ref, k, c_in):
    total = row_pair(ref, k)
    lane = iota((1, total.shape[1]), 1)
    counts = jnp.sum(jnp.where(lane == c_in, total, 0.0), axis=1, keepdims=True)
    total = jnp.where(lane < c_in, total, 0.0)
    return finish_rows(total, counts[0:1]), counts[0:1], counts[1:2]


def back_rows(total, count, gain, inverse):
    outer = gain * inverse
    return outer, outer * inverse * (total[1:2] / count), outer * (total[0:1] / count)


def prepare_weights(conv_first, conv_second, conv_point, vectors, c_lane):
    taps, c_in, c_mid = conv_first.shape
    taps_b, _, c_res = conv_second.shape
    c_pad = up(c_in, 16)
    depth = up(taps * c_pad, TILE)
    room = up(c_pad + (taps - 1) * (c_pad % LANES), LANES)
    base = c_pad - c_pad % LANES
    many = len(vectors)

    def body(info, first, second, point, *rest):
        vector_refs = rest[:many]
        first_out, back_out, second_out, second_back, point_out, table, wide_sum = rest[many:]
        for index, ref in enumerate(vector_refs):
            value = ref[...]
            if value.shape[0] < c_lane:
                value = jnp.pad(value, (0, c_lane - value.shape[0]))
            table[index : index + 1, :] = value.reshape(1, c_lane)
        eye = identity()
        for row in range(0, c_mid, TILE):
            wide_sum[...] = jnp.zeros_like(wide_sum)
            for tap in range(taps):
                turned = nt(eye, first[tap, :, row : row + TILE])
                padded = jnp.concatenate([turned, jnp.zeros((TILE, room - c_in), F32)], axis=1)
                moved = pltpu.roll(padded, tap * (c_pad % LANES), 1) if tap else padded
                wide_sum[:, tap * base : tap * base + room] += moved
            first_out[row : row + TILE, :] = wide_sum[:, :depth].astype(BF16)
        for tap in range(taps):
            back_out[:c_in, tap * c_mid : (tap + 1) * c_mid] = first[tap]
        back_out[c_in:, :] = jnp.zeros((c_pad - c_in, taps * c_mid), BF16)
        eye_res = choose(iota((c_res, c_res), 0) == iota((c_res, c_res), 1)).astype(BF16)
        for tap in range(taps_b):
            second_out[:, tap * c_mid : (tap + 1) * c_mid] = nt(eye_res, second[tap]).astype(BF16)
            second_back[:, tap * c_res : (tap + 1) * c_res] = second[tap]
        eye_mid = choose(iota((c_mid, c_mid), 0) == iota((c_mid, c_mid), 1)).astype(BF16)
        point_out[...] = nt(eye_mid, point[...]).astype(BF16)

    outs = [
        ((c_mid, depth), BF16),
        ((c_pad, taps * c_mid), BF16),
        ((c_res, taps_b * c_mid), BF16),
        ((c_mid, taps_b * c_res), BF16),
        ((c_mid, c_res), BF16),
        ((up(many, 8), c_lane), F32),
    ]
    return call(
        "prepare_weights",
        body,
        (1,),
        [whole(a.shape) for a in (conv_first, conv_second, conv_point, *vectors)],
        [whole(s) for s, _ in outs],
        [shape_of(s, t) for s, t in outs],
        [pltpu.VMEM((TILE, max(depth, (taps - 1) * base + room)), F32)],
    )


def load_features(micro, bins, c_in):
    c_pad = up(c_in, 16)
    c_lane = up(c_in, LANES)
    step = 2 * TILE
    steps = bins // step

    def body(info, f_ref, x_ref, st_ref, own, s_acc, q_acc):
        k, at = pl.program_id(0), pl.program_id(1)
        section, length = info[0], info[1 + k]

        @pl.when(at == 0)
        def _():
            s_acc[...] = jnp.zeros_like(s_acc)
            q_acc[...] = jnp.zeros_like(q_acc)

        @pl.when((at == 0) & (k == 0))
        def _():
            st_ref[...] = jnp.zeros_like(st_ref)

        flat = f_ref[0].reshape(2 * c_in, step)
        spot = iota((TILE, TILE), 1)
        source = jnp.where(spot < LANES, 2 * spot, 2 * spot - (TILE - 1))
        split = choose(iota((TILE, TILE), 0) == source).astype(BF16)
        keep = choose(iota((1, step), 1) + at * step < length)
        for row in range(0, c_in, LANES):
            count = min(LANES, c_in - row)
            count_pad = up(count, 16)
            pick = choose(
                iota((count_pad, 2 * count), 1) == 2 * iota((count_pad, 2 * count), 0) + section
            ).astype(BF16)
            chosen = nn(pick, flat[2 * row : 2 * (row + count)])
            own[row : row + count_pad, :] = (chosen * keep).astype(BF16)
        low = nn(own[:, :TILE], split)
        high = nn(own[:, TILE:], split)
        x_ref[0, 0, :, :LANES] = low[:, :LANES].astype(BF16)
        x_ref[0, 0, :, LANES:] = high[:, :LANES].astype(BF16)
        x_ref[0, 1, :, :LANES] = low[:, LANES:].astype(BF16)
        x_ref[0, 1, :, LANES:] = high[:, LANES:].astype(BF16)
        s_acc[:c_pad, :] += fold(low) + fold(high)
        q_acc[:c_pad, :] += fold(low * low) + fold(high * high)

        @pl.when(at == steps - 1)
        def _():
            lane = iota((1, c_lane), 1)
            count_in = length.astype(F32)
            count_pool = ((length + 1) // 2).astype(F32)
            put_rows(
                st_ref,
                k,
                jnp.where(lane < c_in, as_row(s_acc[...]), count_in),
                jnp.where(lane < c_in, as_row(q_acc[...]), count_pool),
            )

    return call(
        "load_features",
        body,
        (micro, steps),
        [pl.BlockSpec((1, c_in, 2, step), lambda k, j, _: (k, 0, 0, j))],
        [per_lanes((2, c_pad, TILE)), whole((8, c_lane))],
        [shape_of((micro, 2, c_pad, bins // 2), BF16), shape_of((8, c_lane))],
        [pltpu.VMEM((c_pad, step), BF16)] + [pltpu.VMEM((c_lane, LANES), F32)] * 2,
    )


def forward_first(micro, c_in, c_mid, taps, pooled):
    c_pad = up(c_in, 16)
    c_lane = up(c_in, LANES)
    depth = up(taps * c_pad, TILE)
    extra = depth - taps * c_pad
    steps = pooled // TILE
    stack_rows = (taps + 1) * c_pad + extra

    def body(info, x_ref, sums, table, weight, hid, diff, act, st_ref,
             stack, col_c, col_s, col_h, bias, s_acc, q_acc, even, odd):
        k, at = pl.program_id(0), pl.program_id(1)
        length = info[1 + k]

        @pl.when((at == 0) & (k == 0))
        def _():
            stack[(taps + 1) * c_pad :, :] = jnp.zeros((extra, pooled), BF16)
            col_h[...] = column(table[1:2, :])
            bias[...] = column(table[2:3, :c_mid])
            st_ref[...] = jnp.zeros_like(st_ref)

        @pl.when(at == 0)
        def _():
            (centre, _, inverse), _, _ = first_rows(sums, k, c_in)
            col_c[...] = column(centre)
            col_s[...] = column(inverse * table[0:1, :])
            s_acc[...] = jnp.zeros_like(s_acc)
            q_acc[...] = jnp.zeros_like(q_acc)
            masks = pool_mask(length, pooled), odd_mask(length, pooled)

            def rows_body(rows, start):
                c, s, h = (wide(r[rows, :], TILE) for r in (col_c, col_s, col_h))
                here = lambda seg: pl.ds(aligned(seg * c_pad + start), 16)
                for half in range(2):
                    parts = []
                    for lane in range(0, pooled, TILE):
                        lanes = slice(lane, lane + TILE)
                        v = (x_ref[0, half, rows, lanes].astype(F32) - c) * s + h
                        parts.append((gelu(v) * masks[half][:, lanes]).astype(BF16))
                    a = jnp.concatenate(parts, axis=1)
                    act[0, half, rows, :] = a
                    stack[here(half), :] = before(a)
                    stack[here(2 + half), :] = a
                    stack[here(4 + half), :] = after(a)

            each_rows(c_pad, rows_body, 4)

        lanes = pl.ds(pl.multiple_of(at * TILE, TILE), TILE)
        even[...] = nn(weight[...], stack[:depth, lanes])
        odd[...] = nn(weight[...], stack[c_pad : c_pad + depth, lanes])
        mask = pool_mask(length, TILE, at * TILE)

        def rows_body(rows, start):
            b = wide(bias[rows, :], TILE)
            left, right = even[rows, :] + b, odd[rows, :] + b
            apart = left - right
            joined = jnp.maximum(left, right) + jnp.log1p(jnp.exp(-jnp.abs(apart)))
            rounded = (joined * mask).astype(BF16)
            diff[0, rows, :] = apart
            hid[0, rows, :] = rounded
            value = rounded.astype(F32)
            s_acc[rows, :] += fold(value)
            q_acc[rows, :] += fold(value * value)

        each_rows(c_mid, rows_body, 12)

        @pl.when(at == steps - 1)
        def _():
            put_rows(st_ref, k, as_row(s_acc[...]), as_row(q_acc[...]))

    return call(
        "forward_first",
        body,
        (micro, steps),
        [
            per_batch((2, c_pad, pooled)),
            whole((8, c_lane)),
            whole((8, c_lane)),
            whole((c_mid, depth), 1),
        ],
        [
            per_lanes((c_mid, TILE)),
            per_lanes((c_mid, TILE)),
            per_batch((2, c_pad, pooled)),
            whole((8, c_mid)),
        ],
        [
            shape_of((micro, c_mid, pooled), BF16),
            shape_of((micro, c_mid, pooled)),
            shape_of((micro, 2, c_pad, pooled), BF16),
            shape_of((8, c_mid)),
        ],
        [pltpu.VMEM((stack_rows, pooled), BF16)]
        + [pltpu.VMEM((c_lane, LANES), F32)] * 3
        + [pltpu.VMEM((c_mid, LANES), F32)] * 3
        + [pltpu.VMEM((c_mid, TILE), F32)] * 2,
    )


def forward_second(micro, c_in, c_mid, c_res, taps, pooled, c_lane):
    def body(info, hid, sums_a, sums, table, weight, conv, act, st_ref,
             stack, col_c, col_s, col_h, s_acc, q_acc):
        k = pl.program_id(0)
        length = info[1 + k]
        _, _, count = first_rows(sums_a, k, c_in)
        centre, _, inverse = finish_rows(row_pair(sums, k), count)
        col_c[...] = column(centre)
        col_s[...] = column(inverse * table[3:4, :c_mid])

        @pl.when(k == 0)
        def _():
            col_h[...] = column(table[4:5, :c_mid])
            st_ref[...] = jnp.zeros_like(st_ref)

        mask = pool_mask(length, pooled)

        def rows_body(rows, start):
            c, s, h = (wide(r[rows, :], TILE) for r in (col_c, col_s, col_h))
            here = lambda seg: pl.ds(aligned(seg * c_mid + start), 16)
            parts = []
            for lane in range(0, pooled, TILE):
                lanes = slice(lane, lane + TILE)
                v = (hid[0, rows, lanes].astype(F32) - c) * s + h
                parts.append((gelu(v) * mask[:, lanes]).astype(BF16))
            a = jnp.concatenate(parts, axis=1)
            act[0, rows, :] = a
            stack[here(0), :] = before(a)
            stack[here(1), :] = a
            stack[here(2), :] = after(a)

        each_rows(c_mid, rows_body, 8)
        for at in range(0, pooled, TILE):
            conv[0, :, at : at + TILE] = nn(weight[...], stack[:, at : at + TILE])

        def moments_body(rows, start):
            value = conv[0, rows, :] * mask
            s_acc[rows, :] = fold(value)
            q_acc[rows, :] = fold(value * value)

        each_rows(c_res, moments_body, 8)
        put_rows(st_ref, k, as_row(s_acc[...]), as_row(q_acc[...]))

    return call(
        "forward_second",
        body,
        (micro,),
        [
            per_batch((c_mid, pooled)),
            whole((8, c_lane)),
            whole((8, c_mid)),
            whole((8, c_lane)),
            whole((c_res, taps * c_mid), 1),
        ],
        [per_batch((c_res, pooled)), per_batch((c_mid, pooled)), whole((8, c_res))],
        [
            shape_of((micro, c_res, pooled)),
            shape_of((micro, c_mid, pooled), BF16),
            shape_of((8, c_res)),
        ],
        [pltpu.VMEM((taps * c_mid, pooled), BF16)]
        + [pltpu.VMEM((c_mid, LANES), F32)] * 3
        + [pltpu.VMEM((c_res, LANES), F32)] * 2,
    )


def turn_point(micro, c_in, c_mid, c_res, pooled, c_lane):
    half = c_mid // 2

    def body(info, conv, sums_a, sums, table, hid, cot, point_t, point,
             own, send, go, d_out, st_ref, point_own, point_send, grad_bias,
             act, up_grad, branch, flat, bias, col_c, col_s, col_h, s_acc, q_acc, product):
        k = pl.program_id(0)
        section, length = info[0], info[1 + k]
        first = section == 0
        _, _, count = first_rows(sums_a, k, c_in)
        centre, _, inverse = finish_rows(row_pair(sums, k), count)
        col_c[...] = column(centre)
        col_s[...] = column(inverse * table[5:6, :c_res])

        @pl.when(k == 0)
        def _():
            col_h[...] = column(table[6:7, :c_res])
            bias[...] = column(table[7:8, :c_mid])
            product[...] = jnp.zeros_like(product)
            grad_bias[...] = jnp.zeros_like(grad_bias)
            st_ref[...] = jnp.zeros_like(st_ref)

        mask = pool_mask(length, pooled)
        up_grad[...] = nt(point[...], cot[0, 0])

        def rows_body(rows, start):
            c, s, h = (wide(r[rows, :], TILE) for r in (col_c, col_s, col_h))
            total_s, total_q = [], []
            for lane in range(0, pooled, TILE):
                lanes = slice(lane, lane + TILE)
                apart = conv[0, rows, lanes] - c
                a, slope = gelu_slope(apart * s + h)
                act[rows, lanes] = (a * mask[:, lanes]).astype(BF16)
                d = mask[:, lanes] * slope * up_grad[rows, lanes]
                d_out[0, rows, lanes] = d
                total_s.append(fold(d))
                total_q.append(fold(d * apart))
            s_acc[rows, :] = sum(total_s)
            q_acc[rows, :] = sum(total_q)

        each_rows(c_res, rows_body, 4)
        put_rows(st_ref, k, as_row(s_acc[...]), as_row(q_acc[...]) * inverse)
        branch[...] = nn(point_t[...], act[...])

        def out_body(rows, start):
            b = wide(bias[rows, :], pooled)
            total = hid[0, rows, :].astype(F32) + (branch[rows, :] + b)
            flat[rows, :] = (total * mask).astype(BF16)

        each_rows(c_mid, out_body, 8)
        eye = identity()
        for at in range(0, pooled, TILE):
            turned = nt(eye, flat[:, at : at + TILE]).astype(BF16)
            low, high = turned[:, :half], turned[:, half:]
            own[0, at : at + TILE, :] = jnp.where(first, low, high)
            send[0, at : at + TILE, :] = jnp.where(first, high, low)
        for at in range(0, c_mid, TILE):
            go[0, at : at + TILE, :] = (nt(eye, cot[0, 0, :, at : at + TILE]) * mask).astype(BF16)
        product[...] += nn(act[...], cot[0, 0])
        ones = jnp.broadcast_to(mask, (16, pooled)).astype(BF16)
        grad_bias[...] += nn(ones, cot[0, 0])[:8]

        @pl.when(k == micro - 1)
        def _():
            low, high = product[:, :half], product[:, half:]
            point_own[...] = jnp.where(first, low, high)
            point_send[...] = jnp.where(first, high, low).astype(BF16)

    in_specs = [
        per_batch((c_res, pooled)),
        whole((8, c_lane)),
        whole((8, c_res)),
        whole((8, c_lane)),
        per_batch((c_mid, pooled)),
        pl.BlockSpec((1, 1, pooled, c_mid), lambda k, info: (k, info[0], 0, 0)),
        whole((c_mid, c_res), 1),
        whole((c_res, c_mid), 1),
    ]
    return call(
        "turn_point",
        body,
        (micro,),
        in_specs,
        [
            per_batch((pooled, half)),
            per_batch((pooled, half)),
            per_batch((c_mid, pooled)),
            per_batch((c_res, pooled)),
            whole((8, c_res)),
            whole((c_res, half)),
            whole((c_res, half)),
            whole((8, c_mid)),
        ],
        [
            shape_of((micro, pooled, half), BF16),
            shape_of((micro, pooled, half), BF16),
            shape_of((micro, c_mid, pooled), BF16),
            shape_of((micro, c_res, pooled)),
            shape_of((8, c_res)),
            shape_of((c_res, half)),
            shape_of((c_res, half), BF16),
            shape_of((8, c_mid)),
        ],
        [
            pltpu.VMEM((c_res, pooled), BF16),
            pltpu.VMEM((c_res, pooled), F32),
            pltpu.VMEM((c_mid, pooled), F32),
            pltpu.VMEM((c_mid, pooled), BF16),
            pltpu.VMEM((c_mid, LANES), F32),
        ]
        + [pltpu.VMEM((c_res, LANES), F32)] * 5
        + [pltpu.VMEM((c_res, c_mid), F32)],
    )


def backward_second(micro, c_in, c_mid, c_res, taps, pooled, c_lane):
    half = c_mid // 2

    def body(info, d_in, conv, sums_a, sums_b, sums_c, back, table, hid, act, weight,
             d_out, st_ref, conv_own, conv_send,
             stack, up_grad, product, col_a, col_b, col_0, col_r, col_c, col_s, col_h, s_acc, q_acc):
        k = pl.program_id(0)
        length = info[1 + k]
        first = info[0] == 0
        _, _, count = first_rows(sums_a, k, c_in)
        centre, _, inverse = finish_rows(row_pair(sums_c, k), count)
        outer, slant, level = back_rows(row_pair(back, k), count, table[5:6, :c_res], inverse)
        col_a[...] = column(outer)
        col_b[...] = column(slant)
        col_0[...] = column(level)
        col_r[...] = column(centre)
        centre, _, inverse = finish_rows(row_pair(sums_b, k), count)
        col_c[...] = column(centre)
        col_s[...] = column(inverse * table[3:4, :c_mid])

        @pl.when(k == 0)
        def _():
            col_h[...] = column(table[4:5, :c_mid])
            product[...] = jnp.zeros_like(product)
            st_ref[...] = jnp.zeros_like(st_ref)

        mask = pool_mask(length, pooled)

        def rows_body(rows, start):
            a, b, z, c = (wide(r[rows, :], pooled) for r in (col_a, col_b, col_0, col_r))
            g = (a * d_in[0, rows, :] - b * (conv[0, rows, :] - c) - z) * mask
            g = g.astype(BF16)
            here = lambda seg: pl.ds(aligned(seg * c_res + start), 16)
            stack[here(0), :] = after(g)
            stack[here(1), :] = g
            stack[here(2), :] = before(g)

        each_rows(c_res, rows_body, 8)
        for at in range(0, pooled, TILE):
            up_grad[:, at : at + TILE] = nn(weight[...], stack[:, at : at + TILE])

        def slope_body(rows, start):
            c, s, h = (wide(r[rows, :], TILE) for r in (col_c, col_s, col_h))
            total_s, total_q = [], []
            for lane in range(0, pooled, TILE):
                lanes = slice(lane, lane + TILE)
                apart = hid[0, rows, lanes].astype(F32) - c
                _, slope = gelu_slope(apart * s + h)
                d = mask[:, lanes] * slope * up_grad[rows, lanes]
                d_out[0, rows, lanes] = d
                total_s.append(fold(d))
                total_q.append(fold(d * apart))
            s_acc[rows, :] = sum(total_s)
            q_acc[rows, :] = sum(total_q)

        each_rows(c_mid, slope_body, 4)
        put_rows(st_ref, k, as_row(s_acc[...]), as_row(q_acc[...]) * inverse)
        for tap in range(taps):
            product[tap] += nt(act[0], stack[tap * c_res : (tap + 1) * c_res, :])

        @pl.when(k == micro - 1)
        def _():
            for tap in range(taps):
                low, high = product[tap, :half, :], product[tap, half:, :]
                conv_own[tap] = jnp.where(first, low, high)
                conv_send[tap] = jnp.where(first, high, low).astype(BF16)

    in_specs = [
        per_batch((c_res, pooled)),
        per_batch((c_res, pooled)),
        whole((8, c_lane)),
        whole((8, c_mid)),
        whole((8, c_res)),
        whole((8, c_res)),
        whole((8, c_lane)),
        per_batch((c_mid, pooled)),
        per_batch((c_mid, pooled)),
        whole((c_mid, taps * c_res), 1),
    ]
    return call(
        "backward_second",
        body,
        (micro,),
        in_specs,
        [
            per_batch((c_mid, pooled)),
            whole((8, c_mid)),
            whole((taps, half, c_res)),
            whole((taps, half, c_res)),
        ],
        [
            shape_of((micro, c_mid, pooled)),
            shape_of((8, c_mid)),
            shape_of((taps, half, c_res)),
            shape_of((taps, half, c_res), BF16),
        ],
        [
            pltpu.VMEM((taps * c_res, pooled), BF16),
            pltpu.VMEM((c_mid, pooled), F32),
            pltpu.VMEM((taps, c_mid, c_res), F32),
        ]
        + [pltpu.VMEM((c_res, LANES), F32)] * 4
        + [pltpu.VMEM((c_mid, LANES), F32)] * 5,
    )


def stack_gradient(stack, half, here, gradient):
    order = 3 - half
    stack[here(order - 2), :] = after(gradient)
    stack[here(order), :] = gradient
    stack[here(order + 2), :] = before(gradient)


def weights_first(micro, c_in, c_mid, taps, pooled, c_lane):
    c_pad = up(c_in, 16)
    half = c_mid // 2

    def body(info, d_in, hid, go, diff, sums_a, sums_b, back, table, act,
             g_out, bias_out, conv_own, conv_send,
             stack, product, col_a, col_b, col_0, col_c, s_acc):
        k, at = pl.program_id(0), pl.program_id(1)
        length = info[1 + k]
        first = info[0] == 0

        @pl.when((at == 0) & (k == 0))
        def _():
            bias_out[...] = jnp.zeros_like(bias_out)

        @pl.when(at == 0)
        def _():
            _, _, count = first_rows(sums_a, k, c_in)
            centre, _, inverse = finish_rows(row_pair(sums_b, k), count)
            outer, slant, level = back_rows(row_pair(back, k), count, table[3:4, :c_mid], inverse)
            col_a[...] = column(outer)
            col_b[...] = column(slant)
            col_0[...] = column(level)
            col_c[...] = column(centre)
            mask = pool_mask(length, pooled)

            def rows_body(rows, start):
                a, b, z, c = (wide(r[rows, :], TILE) for r in (col_a, col_b, col_0, col_c))
                lefts, rights, totals = [], [], []
                for lane in range(0, pooled, TILE):
                    lanes = slice(lane, lane + TILE)
                    field = a * d_in[0, rows, lanes] - b * (hid[0, rows, lanes].astype(F32) - c) - z
                    g = field * mask[:, lanes] + go[0, rows, lanes].astype(F32)
                    g = g.astype(BF16).astype(F32)
                    apart = diff[0, rows, lanes]
                    small = jnp.exp(-jnp.abs(apart))
                    large = 1.0 / (1.0 + small)
                    small = small * large
                    positive = apart >= 0.0
                    left = (g * jnp.where(positive, large, small)).astype(BF16)
                    right = (g * jnp.where(positive, small, large)).astype(BF16)
                    lefts.append(left)
                    rights.append(right)
                    totals.append(fold(left.astype(F32) + right.astype(F32)))
                s_acc[rows, :] = sum(totals)
                here = lambda seg: pl.ds(aligned(seg * c_mid + start), 16)
                for side, parts in enumerate((lefts, rights)):
                    joined = jnp.concatenate(parts, axis=1)
                    g_out[0, side, rows, :] = joined
                    stack_gradient(stack, side, here, joined)

            each_rows(c_mid, rows_body, 4)
            bias_out[...] += as_row(s_acc[...])

        even = pl.ds(pl.multiple_of((at + 1) * c_mid, c_mid), c_mid)
        odd = pl.ds(pl.multiple_of(at * c_mid, c_mid), c_mid)
        value = nt(act[0, 0], stack[even, :]) + nt(act[0, 1], stack[odd, :])

        @pl.when(k == 0)
        def _():
            product[at] = value

        @pl.when((k > 0) & (k < micro - 1))
        def _():
            product[at] += value

        @pl.when(k == micro - 1)
        def _():
            total = (product[at] + value)[:c_in]
            low, high = total[:, :half], total[:, half:]
            conv_own[0] = jnp.where(first, low, high)
            conv_send[0] = jnp.where(first, high, low).astype(BF16)

    block = pl.BlockSpec(
        (1, c_in, half), lambda k, j, _: (jnp.where(k == micro - 1, j, 0), 0, 0)
    )
    in_specs = [
        per_batch((c_mid, pooled)),
        per_batch((c_mid, pooled)),
        per_batch((c_mid, pooled)),
        per_batch((c_mid, pooled)),
        whole((8, c_lane)),
        whole((8, c_mid)),
        whole((8, c_mid)),
        whole((8, c_lane)),
        per_batch((2, c_pad, pooled)),
    ]
    return call(
        "weights_first",
        body,
        (micro, taps),
        in_specs,
        [per_batch((2, c_mid, pooled)), whole((8, c_mid)), block, block],
        [
            shape_of((micro, 2, c_mid, pooled), BF16),
            shape_of((8, c_mid)),
            shape_of((taps, c_in, half)),
            shape_of((taps, c_in, half), BF16),
        ],
        [pltpu.VMEM(((taps + 1) * c_mid, pooled), BF16), pltpu.VMEM((taps, c_pad, c_mid), F32)]
        + [pltpu.VMEM((c_mid, LANES), F32)] * 5,
    )


def backward_first(micro, c_in, c_mid, taps, pooled, c_lane):
    c_pad = up(c_in, 16)
    steps = pooled // TILE

    def body(info, g_in, x_ref, sums_a, table, weight, bias_first, bias_point, d_out, st_ref,
             stack, even, odd, col_c, col_s, col_h, s_acc, q_acc):
        k, at = pl.program_id(0), pl.program_id(1)
        length = info[1 + k]
        (centre, _, inverse), _, _ = first_rows(sums_a, k, c_in)

        @pl.when((at == 0) & (k == 0))
        def _():
            col_h[...] = column(table[1:2, :])
            st_ref[2 * micro : 2 * micro + 1, :] = bias_first[0:1, :]
            st_ref[2 * micro + 1 : 2 * micro + 2, :] = bias_point[0:1, :]

        @pl.when(at == 0)
        def _():
            col_c[...] = column(centre)
            col_s[...] = column(inverse * table[0:1, :])
            s_acc[...] = jnp.zeros_like(s_acc)
            q_acc[...] = jnp.zeros_like(q_acc)

            def rows_body(rows, start):
                here = lambda seg: pl.ds(aligned(seg * c_mid + start), 16)
                stack_gradient(stack, 0, here, g_in[0, 0, rows, :])
                stack_gradient(stack, 1, here, g_in[0, 1, rows, :])

            each_rows(c_mid, rows_body, 8)

        lanes = pl.ds(pl.multiple_of(at * TILE, TILE), TILE)
        depth = taps * c_mid
        even[...] = nn(weight[...], stack[c_mid : c_mid + depth, lanes])
        odd[...] = nn(weight[...], stack[:depth, lanes])
        masks = pool_mask(length, TILE, at * TILE), odd_mask(length, TILE, at * TILE)

        def rows_body(rows, start):
            c, s, h = (wide(r[rows, :], TILE) for r in (col_c, col_s, col_h))
            for half, upstream in enumerate((even, odd)):
                apart = x_ref[0, half, rows, :].astype(F32) - c
                _, slope = gelu_slope(apart * s + h)
                d = masks[half] * slope * upstream[rows, :]
                d_out[0, half, rows, :] = d
                s_acc[rows, :] += fold(d)
                q_acc[rows, :] += fold(d * apart)

        each_rows(c_pad, rows_body, 10)

        @pl.when(at == steps - 1)
        def _():
            put_rows(st_ref, k, as_row(s_acc[...]), as_row(q_acc[...]) * inverse)

    return call(
        "backward_first",
        body,
        (micro, steps),
        [
            per_batch((2, c_mid, pooled)),
            per_lanes((2, c_pad, TILE)),
            whole((8, c_lane)),
            whole((8, c_lane)),
            whole((c_pad, taps * c_mid), 1),
            whole((8, c_mid)),
            whole((8, c_mid)),
        ],
        [per_lanes((2, c_pad, TILE)), whole((8, c_lane))],
        [shape_of((micro, 2, c_pad, pooled)), shape_of((8, c_lane))],
        [
            pltpu.VMEM(((taps + 1) * c_mid, pooled), BF16),
            pltpu.VMEM((c_pad, TILE), F32),
            pltpu.VMEM((c_pad, TILE), F32),
        ]
        + [pltpu.VMEM((c_lane, LANES), F32)] * 5,
    )


def finish_first(micro, c_in, pooled, c_lane):
    c_pad = up(c_in, 16)
    half_in = c_in // 2
    steps = pooled // TILE

    def body(info, d_in, x_ref, sums_a, back, table, own, send, flat, col_a, col_b, col_0, col_c):
        k, at = pl.program_id(0), pl.program_id(1)
        section, length = info[0], info[1 + k]

        @pl.when(at == 0)
        def _():
            (centre, _, inverse), count, _ = first_rows(sums_a, k, c_in)
            outer, slant, level = back_rows(row_pair(back, k), count, table[0:1, :], inverse)
            col_a[...] = column(outer)
            col_b[...] = column(slant)
            col_0[...] = column(level)
            col_c[...] = column(centre)

        masks = pool_mask(length, TILE, at * TILE), odd_mask(length, TILE, at * TILE)

        def rows_body(rows, start):
            a, b, z, c = (wide(r[rows, :], TILE) for r in (col_a, col_b, col_0, col_c))
            parts = []
            for half in range(2):
                apart = x_ref[0, half, rows, :].astype(F32) - c
                field = (a * d_in[0, half, rows, :] - b * apart - z) * masks[half]
                parts.append(field.astype(BF16))
            for side in range(0, TILE, LANES):
                flat[rows, 2 * side : 2 * side + LANES] = parts[0][:, side : side + LANES]
                flat[rows, 2 * side + LANES : 2 * side + TILE] = parts[1][:, side : side + LANES]

        each_rows(c_pad, rows_body, 10)
        spot = iota((TILE, TILE), 0)
        source = jnp.where(spot < LANES, 2 * spot, 2 * spot - (TILE - 1))
        join = choose(iota((TILE, TILE), 1) == source).astype(BF16)
        for side in range(0, 2 * TILE, TILE):
            natural = nn(flat[:, side : side + TILE], join)
            low, high = natural[:half_in], natural[half_in : 2 * half_in]
            first = section == 0
            own[0, :, side : side + TILE] = jnp.where(first, low, high).astype(BF16)
            send[0, :, side : side + TILE] = jnp.where(first, high, low).astype(BF16)

    half_block = pl.BlockSpec((1, half_in, 2 * TILE), lambda k, j, _: (k, 0, j))
    return call(
        "finish_first",
        body,
        (micro, steps),
        [
            per_lanes((2, c_pad, TILE)),
            per_lanes((2, c_pad, TILE)),
            whole((8, c_lane)),
            whole((8, c_lane)),
            whole((8, c_lane)),
        ],
        [half_block, half_block],
        [shape_of((micro, half_in, 2 * pooled), BF16)] * 2,
        [pltpu.VMEM((c_pad, 2 * TILE), BF16)] + [pltpu.VMEM((c_lane, LANES), F32)] * 4,
    )


def pair_windows(micro, half_in, bins):
    step = 2 * TILE
    steps = bins // step

    def body(info, own, got, out):
        section = info[0]
        for row in range(0, half_in, LANES):
            count = min(LANES, half_in - row)
            at = iota((2 * count, count), 0) - 2 * iota((2 * count, count), 1)
            joined = nn(choose(at == section).astype(BF16), own[0, row : row + count, :])
            joined += nn(choose(at == 1 - section).astype(BF16), got[0, row : row + count, :])
            out[0, row : row + count] = joined.astype(BF16).reshape(count, 2, step)

    block = pl.BlockSpec((1, half_in, step), lambda k, j, _: (k, 0, j))
    return call(
        "pair_windows",
        body,
        (micro, steps),
        [block, block],
        pl.BlockSpec((1, half_in, 2, step), lambda k, j, _: (k, 0, 0, j)),
        shape_of((micro, half_in, 2, bins), BF16),
    )


def small_outputs(micro, c_in, c_mid, c_res, c_lane):
    def body(info, sums_a, sums_b, sums_c, back_a, back_b, back_c, *rest):
        running = rest[:6]
        outs = rest[6:]

        def put(ref, row):
            ref[...] = row.reshape(row.shape[1])[: ref.shape[0]]

        for at, back in enumerate((back_a, back_b, back_c)):
            put(outs[2 * at], sum(back[2 * k + 1 : 2 * k + 2, :] for k in range(micro)))
            put(outs[2 * at + 1], sum(back[2 * k : 2 * k + 1, :] for k in range(micro)))
        put(outs[6], back_a[2 * micro : 2 * micro + 1, :c_mid])
        put(outs[7], back_a[2 * micro + 1 : 2 * micro + 2, :c_mid])
        firsts = [first_rows(sums_a, k, c_in) for k in range(micro)]
        stats = [[f[0] for f in firsts]]
        for sums in (sums_b, sums_c):
            stats.append(
                [finish_rows(sums[2 * k : 2 * k + 2, :], firsts[k][2]) for k in range(micro)]
            )
        for at, history in enumerate(stats):
            for part in range(2):
                lanes = history[0][part].shape[1]
                value = running[2 * at + part][...]
                if value.shape[0] < lanes:
                    value = jnp.pad(value, (0, lanes - value.shape[0]))
                value = value.reshape(1, lanes)
                for k in range(micro):
                    value = (1.0 - MOMENTUM) * value + MOMENTUM * history[k][part]
                put(outs[8 + 2 * at + part], value)

    widths = [c_in] * 2 + [c_mid] * 2 + [c_res] * 2
    shapes = widths + [c_mid, c_mid] + widths
    tables = [(8, c_lane), (8, c_mid), (8, c_res)] * 2
    return call(
        "small_outputs",
        body,
        (1,),
        [whole(s) for s in tables] + [whole((n,)) for n in widths],
        [whole((n,)) for n in shapes],
        [shape_of((n,)) for n in shapes],
    )


def partner(array):
    return lax.ppermute(array, "section", [(0, 1), (1, 0)])


def share(rows):
    devices = lax.axis_size("section") * lax.axis_size("dp")
    bits = [1 << at for at in range(devices.bit_length() - 1)]
    groups = [[bits[-1], bits[0]]]
    rest = bits[1:-1]
    while rest:
        groups.append(rest[:3])
        rest = rest[3:]
    for group in groups:
        masks = [0]
        for bit in group:
            masks += [mask + bit for mask in masks]
        parts = [
            lax.ppermute(rows, BOTH, [(i, i ^ mask) for i in range(devices)]) if mask else rows
            for mask in masks
        ]
        while len(parts) > 1:
            parts = [a + b for a, b in zip(parts[::2], parts[1::2])]
        rows = parts[0]
    return rows


def share_at_once(rows):
    devices = lax.axis_size("section") * lax.axis_size("dp")
    copies = jnp.broadcast_to(rows[None], (devices,) + rows.shape)
    return jnp.sum(lax.all_to_all(copies, BOTH, 0, 0), axis=0)


def shards(
    features,
    lengths,
    gain_first,
    shift_first,
    conv_first,
    bias_first,
    gain_second,
    shift_second,
    conv_second,
    gain_third,
    shift_third,
    conv_point,
    bias_point,
    mean_first,
    variance_first,
    mean_second,
    variance_second,
    mean_third,
    variance_third,
    cotangent,
):
    micro, _, bins, c_in = features.shape
    pooled = bins // 2
    taps, _, c_mid = conv_first.shape
    taps_b, _, c_res = conv_second.shape
    c_lane = up(c_in, LANES)
    section = lax.axis_index("section").astype(jnp.int32)
    lead = section == 0
    own_lengths = jnp.where(lead, lengths[:, 0], lengths[:, 1]).astype(jnp.int32)
    info = jnp.concatenate([section[None], own_lengths])
    feats = features.transpose(0, 3, 1, 2)

    loaded, part = load_features(micro, bins, c_in)(info, feats)
    sums_a = share_at_once(part)
    vectors = (
        gain_first, shift_first, bias_first, gain_second, shift_second, gain_third, shift_third,
        bias_point,
    )
    first_t, first_b, second_t, second_b, point_t, table = prepare_weights(
        conv_first, conv_second, conv_point, vectors, c_lane
    )(info, conv_first, conv_second, conv_point, *vectors)
    hid, diff, act_a, part = forward_first(micro, c_in, c_mid, taps, pooled)(
        info, loaded, sums_a, table, first_t
    )
    sums_b = share(part)
    conv_b, act_b, part = forward_second(micro, c_in, c_mid, c_res, taps_b, pooled, c_lane)(
        info, hid, sums_a, sums_b, table, second_t
    )
    sums_c = share(part)
    own_out, send_out, go, d_c, part, point_own, point_send, grad_bias = turn_point(
        micro, c_in, c_mid, c_res, pooled, c_lane
    )(info, conv_b, sums_a, sums_c, table, hid, cotangent, point_t, conv_point)
    back_c = share(part)
    got_out = partner(send_out)
    d_b, part, second_own, second_send = backward_second(
        micro, c_in, c_mid, c_res, taps_b, pooled, c_lane
    )(info, d_c, conv_b, sums_a, sums_b, sums_c, back_c, table, hid, act_b, second_b)
    back_b = share(part)
    halves = [
        (mine + partner(other)).astype(BF16)
        for mine, other in ((second_own, second_send), (point_own, point_send))
    ]
    half_second, half_point = lax.psum(tuple(halves), "dp")
    g_a, bias_sum, first_own, first_send = weights_first(micro, c_in, c_mid, taps, pooled, c_lane)(
        info, d_b, hid, go, diff, sums_a, sums_b, back_b, table, act_a
    )
    half_first = lax.psum((first_own + partner(first_send)).astype(BF16), "dp")
    d_a, part = backward_first(micro, c_in, c_mid, taps, pooled, c_lane)(
        info, g_a, loaded, sums_a, table, first_b, bias_sum, grad_bias
    )
    back_a = share(part)
    own_in, send_in = finish_first(micro, c_in, pooled, c_lane)(
        info, d_a, loaded, sums_a, back_a, table
    )
    paired = pair_windows(micro, c_in // 2, bins)(info, own_in, partner(send_in))
    input_grad = paired.transpose(0, 2, 3, 1)
    block_output = jnp.stack(
        [jnp.where(lead, own_out, got_out), jnp.where(lead, got_out, own_out)], axis=1
    )
    small = small_outputs(micro, c_in, c_mid, c_res, c_lane)(
        info, sums_a, sums_b, sums_c, back_a, back_b, back_c,
        mean_first, variance_first, mean_second, variance_second, mean_third, variance_third,
    )

    def join(half, axis):
        other = partner(half)
        low, high = jnp.where(lead, half, other), jnp.where(lead, other, half)
        return jnp.concatenate([low, high], axis=axis).astype(F32)

    return (
        block_output,
        input_grad,
        small[0],
        small[1],
        join(half_first, 2),
        small[6],
        small[2],
        small[3],
        join(half_second, 1),
        small[4],
        small[5],
        join(half_point, 1),
        small[7],
        *small[8:],
    )


def solution(mesh):
    wide_spec = P(None, "dp", None, None)
    split_spec = P(None, "dp", None, "section")
    return jax.shard_map(
        shards,
        mesh=mesh,
        in_specs=(wide_spec, P(None, "dp")) + (P(),) * 17 + (wide_spec,),
        out_specs=(split_spec, split_spec) + (P(),) * 17,
        check_vma=False,
    )
```

```python
from math import pi, sqrt

import jax
import jax.numpy as jnp
from jax import lax
from jax.experimental import pallas as pl
from jax.experimental.pallas import tpu as pltpu
from jax.sharding import PartitionSpec as P

EPSILON = 1e-05
MOMENTUM = 0.4
CURVE = sqrt(2.0 / pi)
CUBIC = CURVE * 0.044715
BF16 = jnp.bfloat16
F32 = jnp.float32
LANES = 128
TILE = 256
BOTH = ("section", "dp")


def up(value, step):
    return -(-value // step) * step


def nn(left, right):
    return jnp.dot(left, right, preferred_element_type=F32)


def nt(left, right):
    return lax.dot_general(left, right, (((1,), (1,)), ((), ())), preferred_element_type=F32)


def iota(shape, axis):
    return lax.broadcasted_iota(jnp.int32, shape, axis)


def choose(flag):
    return jnp.where(flag, 1.0, 0.0)


def identity():
    return choose(iota((TILE, TILE), 0) == iota((TILE, TILE), 1)).astype(BF16)


def gelu(v):
    half = 0.5 * v
    return half + half * jnp.tanh(v * (CURVE + CUBIC * (v * v)))


def gelu_slope(v):
    square = v * v
    bent = jnp.tanh(v * (CURVE + CUBIC * square))
    half = 0.5 * v
    slope = (0.5 + 0.5 * bent) + half * (1.0 - bent * bent) * (CURVE + (3.0 * CUBIC) * square)
    return half + half * bent, slope


def column(row):
    return jnp.transpose(jnp.broadcast_to(row, (LANES, row.shape[1])))


def as_row(partial_sums):
    return jnp.sum(jnp.transpose(partial_sums), axis=0, keepdims=True)


def wide(block, lanes):
    return jnp.concatenate([block] * (lanes // LANES), axis=1)


def fold(block):
    parts = [block[:, at : at + LANES] for at in range(0, block.shape[1], LANES)]
    while len(parts) > 1:
        parts = [a + b for a, b in zip(parts[::2], parts[1::2])]
    return parts[0]


def before(block):
    rolled = pltpu.roll(block, 1, 1)
    inner = choose(iota((block.shape[0], LANES), 1) > 0).astype(block.dtype)
    return jnp.concatenate([rolled[:, :LANES] * inner, rolled[:, LANES:]], axis=1)


def after(block):
    last = block.shape[1] - LANES
    rolled = pltpu.roll(block, block.shape[1] - 1, 1)
    inner = choose(iota((block.shape[0], LANES), 1) < LANES - 1).astype(block.dtype)
    return jnp.concatenate([rolled[:, :last], rolled[:, last:] * inner], axis=1)


def aligned(value):
    return value if isinstance(value, int) else pl.multiple_of(value, 16)


def each_rows(total, body, unroll, step=16):
    group = step * unroll
    full = total // group

    def run(index, carry):
        for turn in range(unroll):
            start = pl.multiple_of(index * group + turn * step, step)
            body(pl.ds(start, step), start)
        return carry

    lax.fori_loop(0, full, run, 0)
    for start in range(full * group, total, step):
        body(pl.ds(start, step), start)


def pool_mask(length, lanes, start=0):
    return choose(2 * (iota((1, lanes), 1) + start) < length)


def odd_mask(length, lanes, start=0):
    return choose(2 * (iota((1, lanes), 1) + start) + 1 < length)


def whole(shape, buffered=None):
    zeros = (0,) * len(shape)
    if buffered is None:
        return pl.BlockSpec(shape, lambda *_: zeros)
    return pl.BlockSpec(shape, lambda *_: zeros, pipeline_mode=pl.Buffered(buffered))


def per_batch(shape):
    return pl.BlockSpec((1,) + shape, lambda k, *_: (k,) + (0,) * len(shape))


def per_lanes(shape):
    return pl.BlockSpec((1,) + shape, lambda k, j, _: (k,) + (0,) * (len(shape) - 1) + (j,))


def shape_of(shape, dtype=F32):
    return jax.ShapeDtypeStruct(shape, dtype)


def call(name, body, grid, in_specs, out_specs, out_shape, scratch=(), limit=58, after=0):
    real = len(in_specs) + 1

    def ordered(*refs):
        body(*refs[:real], *refs[real + after :])

    in_specs = list(in_specs) + [pl.BlockSpec(memory_space=pl.ANY)] * after
    return pl.pallas_call(
        ordered,
        grid_spec=pltpu.PrefetchScalarGridSpec(
            num_scalar_prefetch=1,
            grid=grid,
            in_specs=in_specs,
            out_specs=out_specs,
            scratch_shapes=list(scratch),
        ),
        out_shape=out_shape,
        compiler_params=pltpu.CompilerParams(vmem_limit_bytes=limit * 2**20),
        name=name,
    )


def row_pair(ref, k):
    table = ref[...]
    at = iota(table.shape, 0) - 2 * k
    rows = [jnp.sum(jnp.where(at == r, table, 0.0), axis=0, keepdims=True) for r in range(2)]
    return jnp.concatenate(rows, axis=0)


def put_rows(ref, k, first, second):
    table = ref[...]
    at = iota(table.shape, 0) - 2 * k
    ref[...] = jnp.where(at == 0, first, jnp.where(at == 1, second, table))


def finish_rows(total, count):
    centre = total[0:1] / count
    variance = total[1:2] / count - centre * centre
    return centre, variance, lax.rsqrt(variance + EPSILON)


def first_rows(ref, k, c_in):
    total = row_pair(ref, k)
    lane = iota((1, total.shape[1]), 1)
    counts = jnp.sum(jnp.where(lane == c_in, total, 0.0), axis=1, keepdims=True)
    total = jnp.where(lane < c_in, total, 0.0)
    return finish_rows(total, counts[0:1]), counts[0:1], counts[1:2]


def back_rows(total, count, gain, inverse):
    outer = gain * inverse
    return outer, outer * inverse * (total[1:2] / count), outer * (total[0:1] / count)


def prepare_weights(conv_first, conv_second, conv_point, vectors, c_lane):
    taps, c_in, c_mid = conv_first.shape
    taps_b, _, c_res = conv_second.shape
    c_pad = up(c_in, 16)
    depth = up(taps * c_pad, TILE)
    room = up(c_pad + (taps - 1) * (c_pad % LANES), LANES)
    base = c_pad - c_pad % LANES
    many = len(vectors)

    def body(info, first, second, point, *rest):
        vector_refs = rest[:many]
        first_out, back_out, second_out, second_back, point_out, table, wide_sum = rest[many:]
        for index, ref in enumerate(vector_refs):
            value = ref[...]
            if value.shape[0] < c_lane:
                value = jnp.pad(value, (0, c_lane - value.shape[0]))
            table[index : index + 1, :] = value.reshape(1, c_lane)
        eye = identity()
        for row in range(0, c_mid, TILE):
            wide_sum[...] = jnp.zeros_like(wide_sum)
            for tap in range(taps):
                turned = nt(eye, first[tap, :, row : row + TILE])
                padded = jnp.concatenate([turned, jnp.zeros((TILE, room - c_in), F32)], axis=1)
                moved = pltpu.roll(padded, tap * (c_pad % LANES), 1) if tap else padded
                wide_sum[:, tap * base : tap * base + room] += moved
            first_out[row : row + TILE, :] = wide_sum[:, :depth].astype(BF16)
        for tap in range(taps):
            back_out[:c_in, tap * c_mid : (tap + 1) * c_mid] = first[tap]
        back_out[c_in:, :] = jnp.zeros((c_pad - c_in, taps * c_mid), BF16)
        eye_res = choose(iota((c_res, c_res), 0) == iota((c_res, c_res), 1)).astype(BF16)
        for tap in range(taps_b):
            second_out[:, tap * c_mid : (tap + 1) * c_mid] = nt(eye_res, second[tap]).astype(BF16)
            second_back[:, tap * c_res : (tap + 1) * c_res] = second[tap]
        eye_mid = choose(iota((c_mid, c_mid), 0) == iota((c_mid, c_mid), 1)).astype(BF16)
        point_out[...] = nt(eye_mid, point[...]).astype(BF16)

    outs = [
        ((c_mid, depth), BF16),
        ((c_pad, taps * c_mid), BF16),
        ((c_res, taps_b * c_mid), BF16),
        ((c_mid, taps_b * c_res), BF16),
        ((c_mid, c_res), BF16),
        ((up(many, 8), c_lane), F32),
    ]
    return call(
        "prepare_weights",
        body,
        (1,),
        [whole(a.shape) for a in (conv_first, conv_second, conv_point, *vectors)],
        [whole(s) for s, _ in outs],
        [shape_of(s, t) for s, t in outs],
        [pltpu.VMEM((TILE, max(depth, (taps - 1) * base + room)), F32)],
    )


def load_features(micro, bins, c_in):
    c_pad = up(c_in, 16)
    c_lane = up(c_in, LANES)
    step = 2 * TILE
    steps = bins // step

    def body(info, f_ref, x_ref, st_ref, own, s_acc, q_acc):
        k, at = pl.program_id(0), pl.program_id(1)
        section, length = info[0], info[1 + k]

        @pl.when(at == 0)
        def _():
            s_acc[...] = jnp.zeros_like(s_acc)
            q_acc[...] = jnp.zeros_like(q_acc)

        @pl.when((at == 0) & (k == 0))
        def _():
            st_ref[...] = jnp.zeros_like(st_ref)

        flat = f_ref[0].reshape(2 * c_in, step)
        spot = iota((TILE, TILE), 1)
        source = jnp.where(spot < LANES, 2 * spot, 2 * spot - (TILE - 1))
        split = choose(iota((TILE, TILE), 0) == source).astype(BF16)
        keep = choose(iota((1, step), 1) + at * step < length)
        for row in range(0, c_in, LANES):
            count = min(LANES, c_in - row)
            count_pad = up(count, 16)
            pick = choose(
                iota((count_pad, 2 * count), 1) == 2 * iota((count_pad, 2 * count), 0) + section
            ).astype(BF16)
            chosen = nn(pick, flat[2 * row : 2 * (row + count)])
            own[row : row + count_pad, :] = (chosen * keep).astype(BF16)
        low = nn(own[:, :TILE], split)
        high = nn(own[:, TILE:], split)
        x_ref[0, 0, :, :LANES] = low[:, :LANES].astype(BF16)
        x_ref[0, 0, :, LANES:] = high[:, :LANES].astype(BF16)
        x_ref[0, 1, :, :LANES] = low[:, LANES:].astype(BF16)
        x_ref[0, 1, :, LANES:] = high[:, LANES:].astype(BF16)
        s_acc[:c_pad, :] += fold(low) + fold(high)
        q_acc[:c_pad, :] += fold(low * low) + fold(high * high)

        @pl.when(at == steps - 1)
        def _():
            lane = iota((1, c_lane), 1)
            count_in = length.astype(F32)
            count_pool = ((length + 1) // 2).astype(F32)
            put_rows(
                st_ref,
                k,
                jnp.where(lane < c_in, as_row(s_acc[...]), count_in),
                jnp.where(lane < c_in, as_row(q_acc[...]), count_pool),
            )

    return call(
        "load_features",
        body,
        (micro, steps),
        [pl.BlockSpec((1, c_in, 2, step), lambda k, j, _: (k, 0, 0, j))],
        [per_lanes((2, c_pad, TILE)), whole((8, c_lane))],
        [shape_of((micro, 2, c_pad, bins // 2), BF16), shape_of((8, c_lane))],
        [pltpu.VMEM((c_pad, step), BF16)] + [pltpu.VMEM((c_lane, LANES), F32)] * 2,
    )


def activate(micro, c_in, taps, pooled):
    c_pad = up(c_in, 16)
    c_lane = up(c_in, LANES)
    extra = up(taps * c_pad, TILE) - taps * c_pad
    stack_rows = (taps + 1) * c_pad + extra

    def body(info, x_ref, sums, table, stack, col_c, col_s, col_h):
        k = pl.program_id(0)
        length = info[1 + k]
        (centre, _, inverse), _, _ = first_rows(sums, k, c_in)
        col_c[...] = column(centre)
        col_s[...] = column(inverse * table[0:1, :])

        @pl.when(k == 0)
        def _():
            col_h[...] = column(table[1:2, :])

        stack[0, (taps + 1) * c_pad :, :] = jnp.zeros((extra, pooled), BF16)
        masks = pool_mask(length, pooled), odd_mask(length, pooled)

        def rows_body(rows, start):
            c, s, h = (wide(r[rows, :], TILE) for r in (col_c, col_s, col_h))
            here = lambda seg: pl.ds(aligned(seg * c_pad + start), 16)
            for half in range(2):
                parts = []
                for lane in range(0, pooled, TILE):
                    lanes = slice(lane, lane + TILE)
                    v = (x_ref[0, half, rows, lanes].astype(F32) - c) * s + h
                    parts.append((gelu(v) * masks[half][:, lanes]).astype(BF16))
                a = jnp.concatenate(parts, axis=1)
                stack[0, here(half), :] = before(a)
                stack[0, here(2 + half), :] = a
                stack[0, here(4 + half), :] = after(a)

        each_rows(c_pad, rows_body, 8)

    return call(
        "activate",
        body,
        (micro,),
        [per_batch((2, c_pad, pooled)), whole((8, c_lane)), whole((8, c_lane))],
        per_batch((stack_rows, pooled)),
        shape_of((micro, stack_rows, pooled), BF16),
        [pltpu.VMEM((c_lane, LANES), F32)] * 3,
    )


def lane_blocks(shape, steps, last, late):
    def place(s, _):
        s = jnp.maximum(s - 1, 0) if late else jnp.minimum(s, last)
        return (s // steps,) + (0,) * (len(shape) - 1) + (s % steps,)

    return pl.BlockSpec((1,) + shape, place)


def forward_first(micro, c_in, c_mid, taps, pooled):
    c_pad = up(c_in, 16)
    c_lane = up(c_in, LANES)
    depth = up(taps * c_pad, TILE)
    steps = pooled // TILE
    total = micro * steps
    stack_rows = c_pad + depth

    def body(info, stack, table, weight, hid, diff, st_ref, bias, s_acc, q_acc, even, odd):
        step = pl.program_id(0)
        late = jnp.maximum(step - 1, 0)
        k, at = late // steps, late % steps
        mask = pool_mask(info[1 + k], TILE, at * TILE)

        @pl.when(step == 0)
        def _():
            bias[...] = column(table[2:3, :c_mid])
            st_ref[...] = jnp.zeros_like(st_ref)

        @pl.when(at == 0)
        def _():
            s_acc[...] = jnp.zeros_like(s_acc)
            q_acc[...] = jnp.zeros_like(q_acc)

        def finish():
            for start in range(0, c_mid, 16):
                rows = slice(start, start + 16)
                b = wide(bias[rows, :], TILE)
                left, right = even[rows, :] + b, odd[rows, :] + b
                apart = left - right
                joined = jnp.maximum(left, right) + jnp.log1p(jnp.exp(-jnp.abs(apart)))
                rounded = (joined * mask).astype(BF16)
                diff[0, rows, :] = apart
                hid[0, rows, :] = rounded
                value = rounded.astype(F32)
                s_acc[rows, :] += fold(value)
                q_acc[rows, :] += fold(value * value)

        @pl.when(step < total)
        def _():
            finish()
            even[...] = nn(weight[...], stack[0, :depth, :])
            odd[...] = nn(weight[...], stack[0, c_pad : c_pad + depth, :])

        @pl.when(step == total)
        def _():
            finish()

        @pl.when(at == steps - 1)
        def _():
            put_rows(st_ref, k, as_row(s_acc[...]), as_row(q_acc[...]))

    return call(
        "forward_first",
        body,
        (total + 1,),
        [
            lane_blocks((stack_rows, TILE), steps, total - 1, False),
            whole((8, c_lane)),
            whole((c_mid, depth), 1),
        ],
        [
            lane_blocks((c_mid, TILE), steps, total - 1, True),
            lane_blocks((c_mid, TILE), steps, total - 1, True),
            whole((8, c_mid)),
        ],
        [
            shape_of((micro, c_mid, pooled), BF16),
            shape_of((micro, c_mid, pooled)),
            shape_of((8, c_mid)),
        ],
        [pltpu.VMEM((c_mid, LANES), F32)] * 3 + [pltpu.VMEM((c_mid, TILE), F32)] * 2,
    )


def forward_second(micro, c_in, c_mid, c_res, taps, pooled, c_lane):
    def body(info, hid, sums_a, sums, table, weight, conv, act, st_ref,
             stack, col_c, col_s, col_h, s_acc, q_acc):
        k = pl.program_id(0)
        length = info[1 + k]
        _, _, count = first_rows(sums_a, k, c_in)
        centre, _, inverse = finish_rows(row_pair(sums, k), count)
        col_c[...] = column(centre)
        col_s[...] = column(inverse * table[3:4, :c_mid])

        @pl.when(k == 0)
        def _():
            col_h[...] = column(table[4:5, :c_mid])
            st_ref[...] = jnp.zeros_like(st_ref)

        mask = pool_mask(length, pooled)

        def rows_body(rows, start):
            c, s, h = (wide(r[rows, :], TILE) for r in (col_c, col_s, col_h))
            here = lambda seg: pl.ds(aligned(seg * c_mid + start), 16)
            parts = []
            for lane in range(0, pooled, TILE):
                lanes = slice(lane, lane + TILE)
                v = (hid[0, rows, lanes].astype(F32) - c) * s + h
                parts.append((gelu(v) * mask[:, lanes]).astype(BF16))
            a = jnp.concatenate(parts, axis=1)
            act[0, rows, :] = a
            stack[here(0), :] = before(a)
            stack[here(1), :] = a
            stack[here(2), :] = after(a)

        each_rows(c_mid, rows_body, 8)
        for at in range(0, pooled, TILE):
            conv[0, :, at : at + TILE] = nn(weight[...], stack[:, at : at + TILE])

        def moments_body(rows, start):
            value = conv[0, rows, :] * mask
            s_acc[rows, :] = fold(value)
            q_acc[rows, :] = fold(value * value)

        each_rows(c_res, moments_body, 8)
        put_rows(st_ref, k, as_row(s_acc[...]), as_row(q_acc[...]))

    return call(
        "forward_second",
        body,
        (micro,),
        [
            per_batch((c_mid, pooled)),
            whole((8, c_lane)),
            whole((8, c_mid)),
            whole((8, c_lane)),
            whole((c_res, taps * c_mid), 1),
        ],
        [per_batch((c_res, pooled)), per_batch((c_mid, pooled)), whole((8, c_res))],
        [
            shape_of((micro, c_res, pooled)),
            shape_of((micro, c_mid, pooled), BF16),
            shape_of((8, c_res)),
        ],
        [pltpu.VMEM((taps * c_mid, pooled), BF16)]
        + [pltpu.VMEM((c_mid, LANES), F32)] * 3
        + [pltpu.VMEM((c_res, LANES), F32)] * 2,
        after=1,
    )


def turn_cotangent(micro, c_mid, c_res, pooled):
    def body(info, cot, point, go, up_grad, grad_bias):
        k = pl.program_id(0)
        mask = pool_mask(info[1 + k], pooled)
        eye = identity()
        up_grad[0] = nt(point[...], cot[0, 0])
        for at in range(0, c_mid, TILE):
            go[0, at : at + TILE, :] = (nt(eye, cot[0, 0, :, at : at + TILE]) * mask).astype(BF16)
        ones = jnp.broadcast_to(mask, (16, pooled)).astype(BF16)
        total = nn(ones, cot[0, 0])[:8]
        grad_bias[...] = total + jnp.where(k == 0, 0.0, grad_bias[...])

    return call(
        "turn_cotangent",
        body,
        (micro,),
        [
            pl.BlockSpec((1, 1, pooled, c_mid), lambda k, info: (k, info[0], 0, 0)),
            whole((c_res, c_mid), 1),
        ],
        [per_batch((c_mid, pooled)), per_batch((c_res, pooled)), whole((8, c_mid))],
        [
            shape_of((micro, c_mid, pooled), BF16),
            shape_of((micro, c_res, pooled)),
            shape_of((8, c_mid)),
        ],
    )


def norm_third(micro, c_in, c_res, pooled, c_lane):
    def body(info, conv, up_grad, sums_a, sums, table, act, d_out, st_ref,
             col_c, col_s, col_h, s_acc, q_acc):
        k = pl.program_id(0)
        length = info[1 + k]
        _, _, count = first_rows(sums_a, k, c_in)
        centre, _, inverse = finish_rows(row_pair(sums, k), count)
        col_c[...] = column(centre)
        col_s[...] = column(inverse * table[5:6, :c_res])

        @pl.when(k == 0)
        def _():
            col_h[...] = column(table[6:7, :c_res])
            st_ref[...] = jnp.zeros_like(st_ref)

        mask = pool_mask(length, pooled)

        def rows_body(rows, start):
            c, s, h = (wide(r[rows, :], TILE) for r in (col_c, col_s, col_h))
            total_s, total_q = [], []
            for lane in range(0, pooled, TILE):
                lanes = slice(lane, lane + TILE)
                apart = conv[0, rows, lanes] - c
                a, slope = gelu_slope(apart * s + h)
                act[0, rows, lanes] = (a * mask[:, lanes]).astype(BF16)
                d = mask[:, lanes] * slope * up_grad[0, rows, lanes]
                d_out[0, rows, lanes] = d
                total_s.append(fold(d))
                total_q.append(fold(d * apart))
            s_acc[rows, :] = sum(total_s)
            q_acc[rows, :] = sum(total_q)

        each_rows(c_res, rows_body, 8)
        put_rows(st_ref, k, as_row(s_acc[...]), as_row(q_acc[...]) * inverse)

    return call(
        "norm_third",
        body,
        (micro,),
        [
            per_batch((c_res, pooled)),
            per_batch((c_res, pooled)),
            whole((8, c_lane)),
            whole((8, c_res)),
            whole((8, c_lane)),
        ],
        [per_batch((c_res, pooled)), per_batch((c_res, pooled)), whole((8, c_res))],
        [
            shape_of((micro, c_res, pooled), BF16),
            shape_of((micro, c_res, pooled)),
            shape_of((8, c_res)),
        ],
        [pltpu.VMEM((c_res, LANES), F32)] * 5,
    )


def point_output(micro, c_mid, c_res, pooled, c_lane):
    half = c_mid // 2

    def body(info, act, hid, cot, table, point_t, own, send, grad_point,
             branch, flat, bias, product):
        k = pl.program_id(0)
        first = info[0] == 0
        mask = pool_mask(info[1 + k], pooled)

        @pl.when(k == 0)
        def _():
            bias[...] = column(table[7:8, :c_mid])

        branch[...] = nn(point_t[...], act[0])
        total = nn(act[0], cot[0, 0]) + jnp.where(k == 0, 0.0, product[...])
        product[...] = total
        grad_point[...] = total.astype(BF16)

        def out_body(rows, start):
            b = wide(bias[rows, :], pooled)
            value = hid[0, rows, :].astype(F32) + (branch[rows, :] + b)
            flat[rows, :] = (value * mask).astype(BF16)

        each_rows(c_mid, out_body, 8)
        eye = identity()
        for at in range(0, pooled, TILE):
            turned = nt(eye, flat[:, at : at + TILE]).astype(BF16)
            low, high = turned[:, :half], turned[:, half:]
            own[0, at : at + TILE, :] = jnp.where(first, low, high)
            send[0, at : at + TILE, :] = jnp.where(first, high, low)

    return call(
        "point_output",
        body,
        (micro,),
        [
            per_batch((c_res, pooled)),
            per_batch((c_mid, pooled)),
            pl.BlockSpec((1, 1, pooled, c_mid), lambda k, info: (k, info[0], 0, 0)),
            whole((8, c_lane)),
            whole((c_mid, c_res), 1),
        ],
        [per_batch((pooled, half)), per_batch((pooled, half)), whole((c_res, c_mid))],
        [
            shape_of((micro, pooled, half), BF16),
            shape_of((micro, pooled, half), BF16),
            shape_of((c_res, c_mid), BF16),
        ],
        [
            pltpu.VMEM((c_mid, pooled), F32),
            pltpu.VMEM((c_mid, pooled), BF16),
            pltpu.VMEM((c_mid, LANES), F32),
            pltpu.VMEM((c_res, c_mid), F32),
        ],
    )


def backward_second(micro, c_in, c_mid, c_res, taps, pooled, c_lane):
    def body(info, d_in, conv, sums_a, sums_b, sums_c, back, table, hid, weight,
             d_out, st_ref, stack,
             up_grad, col_a, col_b, col_0, col_r, col_c, col_s, col_h, s_acc, q_acc):
        k = pl.program_id(0)
        length = info[1 + k]
        _, _, count = first_rows(sums_a, k, c_in)
        centre, _, inverse = finish_rows(row_pair(sums_c, k), count)
        outer, slant, level = back_rows(row_pair(back, k), count, table[5:6, :c_res], inverse)
        col_a[...] = column(outer)
        col_b[...] = column(slant)
        col_0[...] = column(level)
        col_r[...] = column(centre)
        centre, _, inverse = finish_rows(row_pair(sums_b, k), count)
        col_c[...] = column(centre)
        col_s[...] = column(inverse * table[3:4, :c_mid])

        @pl.when(k == 0)
        def _():
            col_h[...] = column(table[4:5, :c_mid])
            st_ref[...] = jnp.zeros_like(st_ref)

        mask = pool_mask(length, pooled)

        def rows_body(rows, start):
            a, b, z, c = (wide(r[rows, :], pooled) for r in (col_a, col_b, col_0, col_r))
            g = (a * d_in[0, rows, :] - b * (conv[0, rows, :] - c) - z) * mask
            g = g.astype(BF16)
            here = lambda seg: pl.ds(aligned(seg * c_res + start), 16)
            stack[0, here(0), :] = after(g)
            stack[0, here(1), :] = g
            stack[0, here(2), :] = before(g)

        each_rows(c_res, rows_body, 8)
        for at in range(0, pooled, TILE):
            up_grad[:, at : at + TILE] = nn(weight[...], stack[0, :, at : at + TILE])

        def slope_body(rows, start):
            c, s, h = (wide(r[rows, :], TILE) for r in (col_c, col_s, col_h))
            total_s, total_q = [], []
            for lane in range(0, pooled, TILE):
                lanes = slice(lane, lane + TILE)
                apart = hid[0, rows, lanes].astype(F32) - c
                _, slope = gelu_slope(apart * s + h)
                d = mask[:, lanes] * slope * up_grad[rows, lanes]
                d_out[0, rows, lanes] = d
                total_s.append(fold(d))
                total_q.append(fold(d * apart))
            s_acc[rows, :] = sum(total_s)
            q_acc[rows, :] = sum(total_q)

        each_rows(c_mid, slope_body, 8)
        put_rows(st_ref, k, as_row(s_acc[...]), as_row(q_acc[...]) * inverse)

    in_specs = [
        per_batch((c_res, pooled)),
        per_batch((c_res, pooled)),
        whole((8, c_lane)),
        whole((8, c_mid)),
        whole((8, c_res)),
        whole((8, c_res)),
        whole((8, c_lane)),
        per_batch((c_mid, pooled)),
        whole((c_mid, taps * c_res), 1),
    ]
    return call(
        "backward_second",
        body,
        (micro,),
        in_specs,
        [per_batch((c_mid, pooled)), whole((8, c_mid)), per_batch((taps * c_res, pooled))],
        [
            shape_of((micro, c_mid, pooled)),
            shape_of((8, c_mid)),
            shape_of((micro, taps * c_res, pooled), BF16),
        ],
        [pltpu.VMEM((c_mid, pooled), F32)]
        + [pltpu.VMEM((c_res, LANES), F32)] * 4
        + [pltpu.VMEM((c_mid, LANES), F32)] * 5,
        after=1,
    )


def weights_second(micro, c_mid, c_res, taps, pooled):
    def body(info, act, stack, grad_conv, product):
        k = pl.program_id(0)
        for tap in range(taps):
            value = nt(act[0], stack[0, tap * c_res : (tap + 1) * c_res, :])
            value += jnp.where(k == 0, 0.0, product[tap])
            product[tap] = value
            grad_conv[tap] = value.astype(BF16)

    return call(
        "weights_second",
        body,
        (micro,),
        [per_batch((c_mid, pooled)), per_batch((taps * c_res, pooled))],
        whole((taps, c_mid, c_res)),
        shape_of((taps, c_mid, c_res), BF16),
        [pltpu.VMEM((taps, c_mid, c_res), F32)],
    )


def gradient_first(micro, c_in, c_mid, taps, pooled, c_lane):
    def body(info, d_in, hid, go, diff, sums_a, sums_b, back, table,
             stack, bias_out, col_a, col_b, col_0, col_c, s_acc):
        k = pl.program_id(0)
        length = info[1 + k]
        _, _, count = first_rows(sums_a, k, c_in)
        centre, _, inverse = finish_rows(row_pair(sums_b, k), count)
        outer, slant, level = back_rows(row_pair(back, k), count, table[3:4, :c_mid], inverse)
        col_a[...] = column(outer)
        col_b[...] = column(slant)
        col_0[...] = column(level)
        col_c[...] = column(centre)
        mask = pool_mask(length, pooled)

        def rows_body(rows, start):
            a, b, z, c = (wide(r[rows, :], TILE) for r in (col_a, col_b, col_0, col_c))
            lefts, rights, totals = [], [], []
            for lane in range(0, pooled, TILE):
                lanes = slice(lane, lane + TILE)
                field = a * d_in[0, rows, lanes] - b * (hid[0, rows, lanes].astype(F32) - c) - z
                g = field * mask[:, lanes] + go[0, rows, lanes].astype(F32)
                g = g.astype(BF16).astype(F32)
                apart = diff[0, rows, lanes]
                small = jnp.exp(-jnp.abs(apart))
                large = 1.0 / (1.0 + small)
                small = small * large
                positive = apart >= 0.0
                left = (g * jnp.where(positive, large, small)).astype(BF16)
                right = (g * jnp.where(positive, small, large)).astype(BF16)
                lefts.append(left)
                rights.append(right)
                totals.append(fold(left.astype(F32) + right.astype(F32)))
            s_acc[rows, :] = sum(totals)
            here = lambda seg: pl.ds(aligned(seg * c_mid + start), 16)
            for side, parts in enumerate((lefts, rights)):
                joined = jnp.concatenate(parts, axis=1)
                order = 3 - side
                stack[0, here(order - 2), :] = after(joined)
                stack[0, here(order), :] = joined
                stack[0, here(order + 2), :] = before(joined)

        each_rows(c_mid, rows_body, 6)
        bias_out[...] = as_row(s_acc[...]) + jnp.where(k == 0, 0.0, bias_out[...])

    rows = (taps + 1) * c_mid
    in_specs = [
        per_batch((c_mid, pooled)),
        per_batch((c_mid, pooled)),
        per_batch((c_mid, pooled)),
        per_batch((c_mid, pooled)),
        whole((8, c_lane)),
        whole((8, c_mid)),
        whole((8, c_mid)),
        whole((8, c_lane)),
    ]
    return call(
        "gradient_first",
        body,
        (micro,),
        in_specs,
        [per_batch((rows, pooled)), whole((8, c_mid))],
        [shape_of((micro, rows, pooled), BF16), shape_of((8, c_mid))],
        [pltpu.VMEM((c_mid, LANES), F32)] * 5,
        after=1,
    )


def weights_first(micro, c_in, c_mid, pooled, tap_from, tap_to):
    c_pad = up(c_in, 16)
    count = tap_to - tap_from

    def body(info, act_left, act_right, left, right, grad_conv, product):
        k, at = pl.program_id(0), pl.program_id(1)
        value = nt(act_left[0], left[0]) + nt(act_right[0], right[0])
        value += jnp.where(k == 0, 0.0, product[at])
        product[at] = value
        grad_conv[0] = value[:c_in].astype(BF16)

    def act_block(shift):
        return pl.BlockSpec((1, c_pad, pooled), lambda k, j, _: (k, j + tap_from + shift, 0))

    def grad_block(segment):
        return pl.BlockSpec((1, c_mid, pooled), lambda k, j, _: (k, segment, 0))

    return call(
        "weights_first",
        body,
        (micro, count),
        [act_block(0), act_block(1), grad_block(3), grad_block(2)],
        pl.BlockSpec(
            (1, c_in, c_mid), lambda k, j, _: (jnp.where(k == micro - 1, j, 0), 0, 0)
        ),
        shape_of((count, c_in, c_mid), BF16),
        [pltpu.VMEM((count, c_pad, c_mid), F32)],
        after=1,
    )


def backward_first(micro, c_in, c_mid, taps, pooled, c_lane):
    c_pad = up(c_in, 16)
    steps = pooled // TILE
    total = micro * steps
    depth = taps * c_mid

    def body(info, stack, x_ref, sums_a, table, weight, bias_first, bias_point, d_out, st_ref,
             even, odd, col_c, col_s, col_h, s_acc, q_acc):
        step = pl.program_id(0)
        late = jnp.maximum(step - 1, 0)
        k, at = late // steps, late % steps
        length = info[1 + k]
        (centre, _, inverse), _, _ = first_rows(sums_a, k, c_in)
        masks = pool_mask(length, TILE, at * TILE), odd_mask(length, TILE, at * TILE)

        @pl.when(step == 0)
        def _():
            col_h[...] = column(table[1:2, :])
            st_ref[...] = jnp.zeros_like(st_ref)
            st_ref[2 * micro : 2 * micro + 1, :] = bias_first[0:1, :]
            st_ref[2 * micro + 1 : 2 * micro + 2, :] = bias_point[0:1, :]

        @pl.when(at == 0)
        def _():
            col_c[...] = column(centre)
            col_s[...] = column(inverse * table[0:1, :])
            s_acc[...] = jnp.zeros_like(s_acc)
            q_acc[...] = jnp.zeros_like(q_acc)

        def finish():
            for start in range(0, c_pad, 16):
                rows = slice(start, start + 16)
                c, s, h = (wide(r[rows, :], TILE) for r in (col_c, col_s, col_h))
                for half, upstream in enumerate((even, odd)):
                    apart = x_ref[0, half, rows, :].astype(F32) - c
                    _, slope = gelu_slope(apart * s + h)
                    d = masks[half] * slope * upstream[rows, :]
                    d_out[0, half, rows, :] = d
                    s_acc[rows, :] += fold(d)
                    q_acc[rows, :] += fold(d * apart)

        @pl.when(step < total)
        def _():
            finish()
            even[...] = nn(weight[...], stack[0, c_mid : c_mid + depth, :])
            odd[...] = nn(weight[...], stack[0, :depth, :])

        @pl.when(step == total)
        def _():
            finish()

        @pl.when(at == steps - 1)
        def _():
            put_rows(st_ref, k, as_row(s_acc[...]), as_row(q_acc[...]) * inverse)

    return call(
        "backward_first",
        body,
        (total + 1,),
        [
            lane_blocks((depth + c_mid, TILE), steps, total - 1, False),
            lane_blocks((2, c_pad, TILE), steps, total - 1, True),
            whole((8, c_lane)),
            whole((8, c_lane)),
            whole((c_pad, taps * c_mid), 1),
            whole((8, c_mid)),
            whole((8, c_mid)),
        ],
        [lane_blocks((2, c_pad, TILE), steps, total - 1, True), whole((8, c_lane))],
        [shape_of((micro, 2, c_pad, pooled)), shape_of((8, c_lane))],
        [pltpu.VMEM((c_pad, TILE), F32)] * 2 + [pltpu.VMEM((c_lane, LANES), F32)] * 5,
        after=1,
    )


def finish_first(micro, c_in, pooled, c_lane):
    c_pad = up(c_in, 16)
    half_in = c_in // 2
    steps = pooled // TILE

    def body(info, d_in, x_ref, sums_a, back, table, own, send, flat, col_a, col_b, col_0, col_c):
        k, at = pl.program_id(0), pl.program_id(1)
        section, length = info[0], info[1 + k]

        @pl.when(at == 0)
        def _():
            (centre, _, inverse), count, _ = first_rows(sums_a, k, c_in)
            outer, slant, level = back_rows(row_pair(back, k), count, table[0:1, :], inverse)
            col_a[...] = column(outer)
            col_b[...] = column(slant)
            col_0[...] = column(level)
            col_c[...] = column(centre)

        masks = pool_mask(length, TILE, at * TILE), odd_mask(length, TILE, at * TILE)

        def rows_body(rows, start):
            a, b, z, c = (wide(r[rows, :], TILE) for r in (col_a, col_b, col_0, col_c))
            parts = []
            for half in range(2):
                apart = x_ref[0, half, rows, :].astype(F32) - c
                field = (a * d_in[0, half, rows, :] - b * apart - z) * masks[half]
                parts.append(field.astype(BF16))
            for side in range(0, TILE, LANES):
                flat[rows, 2 * side : 2 * side + LANES] = parts[0][:, side : side + LANES]
                flat[rows, 2 * side + LANES : 2 * side + TILE] = parts[1][:, side : side + LANES]

        each_rows(c_pad, rows_body, 10)
        spot = iota((TILE, TILE), 0)
        source = jnp.where(spot < LANES, 2 * spot, 2 * spot - (TILE - 1))
        join = choose(iota((TILE, TILE), 1) == source).astype(BF16)
        for side in range(0, 2 * TILE, TILE):
            natural = nn(flat[:, side : side + TILE], join)
            low, high = natural[:half_in], natural[half_in : 2 * half_in]
            first = section == 0
            own[0, :, side : side + TILE] = jnp.where(first, low, high).astype(BF16)
            send[0, :, side : side + TILE] = jnp.where(first, high, low).astype(BF16)

    half_block = pl.BlockSpec((1, half_in, 2 * TILE), lambda k, j, _: (k, 0, j))
    return call(
        "finish_first",
        body,
        (micro, steps),
        [
            per_lanes((2, c_pad, TILE)),
            per_lanes((2, c_pad, TILE)),
            whole((8, c_lane)),
            whole((8, c_lane)),
            whole((8, c_lane)),
        ],
        [half_block, half_block],
        [shape_of((micro, half_in, 2 * pooled), BF16)] * 2,
        [pltpu.VMEM((c_pad, 2 * TILE), BF16)] + [pltpu.VMEM((c_lane, LANES), F32)] * 4,
    )


def pair_windows(micro, half_in, bins):
    step = 2 * TILE
    steps = bins // step

    def body(info, own, got, out):
        section = info[0]
        for row in range(0, half_in, LANES):
            count = min(LANES, half_in - row)
            at = iota((2 * count, count), 0) - 2 * iota((2 * count, count), 1)
            joined = nn(choose(at == section).astype(BF16), own[0, row : row + count, :])
            joined += nn(choose(at == 1 - section).astype(BF16), got[0, row : row + count, :])
            out[0, row : row + count] = joined.astype(BF16).reshape(count, 2, step)

    block = pl.BlockSpec((1, half_in, step), lambda k, j, _: (k, 0, j))
    return call(
        "pair_windows",
        body,
        (micro, steps),
        [block, block],
        pl.BlockSpec((1, half_in, 2, step), lambda k, j, _: (k, 0, 0, j)),
        shape_of((micro, half_in, 2, bins), BF16),
    )


def small_outputs(micro, c_in, c_mid, c_res, c_lane):
    def body(info, sums_a, sums_b, sums_c, back_a, back_b, back_c, *rest):
        running = rest[:6]
        outs = rest[6:]

        def put(ref, row):
            ref[...] = row.reshape(row.shape[1])[: ref.shape[0]]

        for at, back in enumerate((back_a, back_b, back_c)):
            put(outs[2 * at], sum(back[2 * k + 1 : 2 * k + 2, :] for k in range(micro)))
            put(outs[2 * at + 1], sum(back[2 * k : 2 * k + 1, :] for k in range(micro)))
        put(outs[6], back_a[2 * micro : 2 * micro + 1, :c_mid])
        put(outs[7], back_a[2 * micro + 1 : 2 * micro + 2, :c_mid])
        firsts = [first_rows(sums_a, k, c_in) for k in range(micro)]
        stats = [[f[0] for f in firsts]]
        for sums in (sums_b, sums_c):
            stats.append(
                [finish_rows(sums[2 * k : 2 * k + 2, :], firsts[k][2]) for k in range(micro)]
            )
        for at, history in enumerate(stats):
            for part in range(2):
                lanes = history[0][part].shape[1]
                value = running[2 * at + part][...]
                if value.shape[0] < lanes:
                    value = jnp.pad(value, (0, lanes - value.shape[0]))
                value = value.reshape(1, lanes)
                for k in range(micro):
                    value = (1.0 - MOMENTUM) * value + MOMENTUM * history[k][part]
                put(outs[8 + 2 * at + part], value)

    widths = [c_in] * 2 + [c_mid] * 2 + [c_res] * 2
    shapes = widths + [c_mid, c_mid] + widths
    tables = [(8, c_lane), (8, c_mid), (8, c_res)] * 2
    return call(
        "small_outputs",
        body,
        (1,),
        [whole(s) for s in tables] + [whole((n,)) for n in widths],
        [whole((n,)) for n in shapes],
        [shape_of((n,)) for n in shapes],
    )


def partner(array):
    return lax.ppermute(array, "section", [(0, 1), (1, 0)])


def share(rows):
    devices = lax.axis_size("section") * lax.axis_size("dp")
    bits = [1 << at for at in range(devices.bit_length() - 1)]
    groups = [[bits[-1], bits[0]]]
    rest = bits[1:-1]
    while rest:
        groups.append(rest[:2])
        rest = rest[2:]
    for group in groups:
        masks = [0]
        for bit in group:
            masks += [mask + bit for mask in masks]
        parts = [
            lax.ppermute(rows, BOTH, [(i, i ^ mask) for i in range(devices)]) if mask else rows
            for mask in masks
        ]
        while len(parts) > 1:
            parts = [a + b for a, b in zip(parts[::2], parts[1::2])]
        rows = parts[0]
    return rows


def shards(
    features,
    lengths,
    gain_first,
    shift_first,
    conv_first,
    bias_first,
    gain_second,
    shift_second,
    conv_second,
    gain_third,
    shift_third,
    conv_point,
    bias_point,
    mean_first,
    variance_first,
    mean_second,
    variance_second,
    mean_third,
    variance_third,
    cotangent,
):
    micro, _, bins, c_in = features.shape
    pooled = bins // 2
    taps, _, c_mid = conv_first.shape
    taps_b, _, c_res = conv_second.shape
    c_lane = up(c_in, LANES)
    section = lax.axis_index("section").astype(jnp.int32)
    lead = section == 0
    own_lengths = jnp.where(lead, lengths[:, 0], lengths[:, 1]).astype(jnp.int32)
    info = jnp.concatenate([section[None], own_lengths])
    feats = features.transpose(0, 3, 1, 2)

    loaded, part = load_features(micro, bins, c_in)(info, feats)
    sums_a = share(part)
    vectors = (
        gain_first, shift_first, bias_first, gain_second, shift_second, gain_third, shift_third,
        bias_point,
    )
    first_t, first_b, second_t, second_b, point_t, table = prepare_weights(
        conv_first, conv_second, conv_point, vectors, c_lane
    )(info, conv_first, conv_second, conv_point, *vectors)
    act_a = activate(micro, c_in, taps, pooled)(info, loaded, sums_a, table)
    hid, diff, part = forward_first(micro, c_in, c_mid, taps, pooled)(info, act_a, table, first_t)
    sums_b = share(part)
    go, up_c, grad_bias = turn_cotangent(micro, c_mid, c_res, pooled)(info, cotangent, conv_point)
    conv_b, act_b, part = forward_second(micro, c_in, c_mid, c_res, taps_b, pooled, c_lane)(
        info, hid, sums_a, sums_b, table, second_t, grad_bias
    )
    sums_c = share(part)
    act_c, d_c, part = norm_third(micro, c_in, c_res, pooled, c_lane)(
        info, conv_b, up_c, sums_a, sums_c, table
    )
    back_c = share(part)
    own_out, send_out, grad_point = point_output(micro, c_mid, c_res, pooled, c_lane)(
        info, act_c, hid, cotangent, table, point_t
    )
    got_out = partner(send_out)
    d_b, part, stack_b = backward_second(micro, c_in, c_mid, c_res, taps_b, pooled, c_lane)(
        info, d_c, conv_b, sums_a, sums_b, sums_c, back_c, table, hid, second_b, grad_point
    )
    back_b = share(part)
    grad_second = weights_second(micro, c_mid, c_res, taps_b, pooled)(info, act_b, stack_b)
    sum_second, sum_point = lax.psum((grad_second, grad_point), BOTH)
    stack_a, bias_sum = gradient_first(micro, c_in, c_mid, taps, pooled, c_lane)(
        info, d_b, hid, go, diff, sums_a, sums_b, back_b, table, grad_second
    )
    cut = taps - taps // 2
    lower = weights_first(micro, c_in, c_mid, pooled, 0, cut)(
        info, act_a, act_a, stack_a, stack_a, bias_sum
    )
    upper = weights_first(micro, c_in, c_mid, pooled, cut, taps)(
        info, act_a, act_a, stack_a, stack_a, lower
    )
    lower, _, _ = lax.optimization_barrier((lower, sum_second, sum_point))
    sum_lower = lax.psum(lower, BOTH)
    sum_upper = lax.psum(upper, BOTH[::-1])
    d_a, part = backward_first(micro, c_in, c_mid, taps, pooled, c_lane)(
        info, stack_a, loaded, sums_a, table, first_b, bias_sum, grad_bias, upper
    )
    back_a = share(part)
    own_in, send_in = finish_first(micro, c_in, pooled, c_lane)(
        info, d_a, loaded, sums_a, back_a, table
    )
    paired = pair_windows(micro, c_in // 2, bins)(info, own_in, partner(send_in))
    input_grad = paired.transpose(0, 2, 3, 1)
    block_output = jnp.stack(
        [jnp.where(lead, own_out, got_out), jnp.where(lead, got_out, own_out)], axis=1
    )
    small = small_outputs(micro, c_in, c_mid, c_res, c_lane)(
        info, sums_a, sums_b, sums_c, back_a, back_b, back_c,
        mean_first, variance_first, mean_second, variance_second, mean_third, variance_third,
    )

    return (
        block_output,
        input_grad,
        small[0],
        small[1],
        jnp.concatenate([sum_lower, sum_upper]).astype(F32),
        small[6],
        small[2],
        small[3],
        sum_second.astype(F32),
        small[4],
        small[5],
        sum_point.astype(F32),
        small[7],
        *small[8:],
    )


def solution(mesh):
    wide_spec = P(None, "dp", None, None)
    split_spec = P(None, "dp", None, "section")
    return jax.shard_map(
        shards,
        mesh=mesh,
        in_specs=(wide_spec, P(None, "dp")) + (P(),) * 17 + (wide_spec,),
        out_specs=(split_spec, split_spec) + (P(),) * 17,
        check_vma=False,
    )
```

```python
from math import pi, sqrt

import jax
import jax.numpy as jnp
from jax import lax
from jax.experimental import pallas as pl
from jax.experimental.pallas import tpu as pltpu
from jax.sharding import PartitionSpec as P

EPSILON = 1e-05
MOMENTUM = 0.4
CURVE = sqrt(2.0 / pi)
CUBIC = CURVE * 0.044715
BF16 = jnp.bfloat16
F32 = jnp.float32
LANES = 128
TILE = 256
STEP = 512
BOTH = ("section", "dp")


def up(value, step):
    return -(-value // step) * step


def nn(left, right):
    return jnp.dot(left, right, preferred_element_type=F32)


def nt(left, right):
    return lax.dot_general(left, right, (((1,), (1,)), ((), ())), preferred_element_type=F32)


def iota(shape, axis):
    return lax.broadcasted_iota(jnp.int32, shape, axis)


def choose(flag):
    return jnp.where(flag, 1.0, 0.0)


def identity():
    return choose(iota((TILE, TILE), 0) == iota((TILE, TILE), 1)).astype(BF16)


def gelu(v):
    half = 0.5 * v
    return half + half * jnp.tanh(v * (CURVE + CUBIC * (v * v)))


def gelu_slope(v):
    square = v * v
    bent = jnp.tanh(v * (CURVE + CUBIC * square))
    half = 0.5 * v
    slope = (0.5 + 0.5 * bent) + half * (1.0 - bent * bent) * (CURVE + (3.0 * CUBIC) * square)
    return half + half * bent, slope


def column(row):
    return jnp.transpose(jnp.broadcast_to(row, (LANES, row.shape[1])))


def as_row(partial_sums):
    return jnp.sum(jnp.transpose(partial_sums), axis=0, keepdims=True)


def wide(block, lanes):
    return jnp.concatenate([block] * (lanes // LANES), axis=1)


def fold(block):
    parts = [block[:, at : at + LANES] for at in range(0, block.shape[1], LANES)]
    while len(parts) > 1:
        parts = [a + b for a, b in zip(parts[::2], parts[1::2])]
    return parts[0]


def before(block):
    rolled = pltpu.roll(block, 1, 1)
    inner = choose(iota((block.shape[0], LANES), 1) > 0).astype(block.dtype)
    return jnp.concatenate([rolled[:, :LANES] * inner, rolled[:, LANES:]], axis=1)


def after(block):
    last = block.shape[1] - LANES
    rolled = pltpu.roll(block, block.shape[1] - 1, 1)
    inner = choose(iota((block.shape[0], LANES), 1) < LANES - 1).astype(block.dtype)
    return jnp.concatenate([rolled[:, :last], rolled[:, last:] * inner], axis=1)


def aligned(value):
    return value if isinstance(value, int) else pl.multiple_of(value, 16)


def each_rows(total, body, unroll, step=16):
    group = step * unroll
    full = total // group

    def run(index, carry):
        for turn in range(unroll):
            start = pl.multiple_of(index * group + turn * step, step)
            body(pl.ds(start, step), start)
        return carry

    lax.fori_loop(0, full, run, 0)
    for start in range(full * group, total, step):
        body(pl.ds(start, step), start)


def pool_mask(length, lanes, start=0):
    return choose(2 * (iota((1, lanes), 1) + start) < length)


def odd_mask(length, lanes, start=0):
    return choose(2 * (iota((1, lanes), 1) + start) + 1 < length)


def whole(shape, buffered=None):
    zeros = (0,) * len(shape)
    if buffered is None:
        return pl.BlockSpec(shape, lambda *_: zeros)
    return pl.BlockSpec(shape, lambda *_: zeros, pipeline_mode=pl.Buffered(buffered))


def per_batch(shape):
    return pl.BlockSpec((1,) + shape, lambda k, *_: (k,) + (0,) * len(shape))


def per_lanes(shape):
    return pl.BlockSpec((1,) + shape, lambda k, j, _: (k,) + (0,) * (len(shape) - 1) + (j,))


def shape_of(shape, dtype=F32):
    return jax.ShapeDtypeStruct(shape, dtype)


def call(name, body, grid, in_specs, out_specs, out_shape, scratch=(), limit=58, after=0):

    real = len(in_specs) + 1

    def ordered(*refs):
        body(*refs[:real], *refs[real + after :])

    in_specs = list(in_specs) + [pl.BlockSpec(memory_space=pl.ANY)] * after
    return pl.pallas_call(
        ordered,
        grid_spec=pltpu.PrefetchScalarGridSpec(
            num_scalar_prefetch=1,
            grid=grid,
            in_specs=in_specs,
            out_specs=out_specs,
            scratch_shapes=list(scratch),
        ),
        out_shape=out_shape,
        compiler_params=pltpu.CompilerParams(vmem_limit_bytes=limit * 2**20),
        name=name,
    )


def row_pair(ref, k):
    table = ref[...]
    at = iota(table.shape, 0) - 2 * k
    rows = [jnp.sum(jnp.where(at == r, table, 0.0), axis=0, keepdims=True) for r in range(2)]
    return jnp.concatenate(rows, axis=0)


def put_rows(ref, k, first, second):
    table = ref[...]
    at = iota(table.shape, 0) - 2 * k
    ref[...] = jnp.where(at == 0, first, jnp.where(at == 1, second, table))


def finish_rows(total, count):
    centre = total[0:1] / count
    variance = total[1:2] / count - centre * centre
    return centre, variance, lax.rsqrt(variance + EPSILON)


def first_rows(ref, k, c_in):
    total = row_pair(ref, k)
    lane = iota((1, total.shape[1]), 1)
    counts = jnp.sum(jnp.where(lane == c_in, total, 0.0), axis=1, keepdims=True)
    total = jnp.where(lane < c_in, total, 0.0)
    return finish_rows(total, counts[0:1]), counts[0:1], counts[1:2]


def back_rows(total, count, gain, inverse):
    outer = gain * inverse
    return outer, outer * inverse * (total[1:2] / count), outer * (total[0:1] / count)


def prepare_table(vectors, c_lane):
    many = len(vectors)

    def body(info, *refs):
        table = refs[many]
        for index, ref in enumerate(refs[:many]):
            value = ref[...]
            if value.shape[0] < c_lane:
                value = jnp.pad(value, (0, c_lane - value.shape[0]))
            table[index : index + 1, :] = value.reshape(1, c_lane)

    return call(
        "prepare_table",
        body,
        (1,),
        [whole(a.shape) for a in vectors],
        whole((up(many, 8), c_lane)),
        shape_of((up(many, 8), c_lane)),
    )


def load_features(micro, bins, c_in):
    c_pad = up(c_in, 16)
    c_lane = up(c_in, LANES)
    step = 2 * TILE
    steps = bins // step

    def body(info, f_ref, x_ref, st_ref, own, s_acc, q_acc):
        k, at = pl.program_id(0), pl.program_id(1)
        section, length = info[0], info[1 + k]

        @pl.when(at == 0)
        def _():
            s_acc[...] = jnp.zeros_like(s_acc)
            q_acc[...] = jnp.zeros_like(q_acc)

        @pl.when((at == 0) & (k == 0))
        def _():
            st_ref[...] = jnp.zeros_like(st_ref)

        flat = f_ref[0].reshape(2 * c_in, step)
        spot = iota((TILE, TILE), 1)
        source = jnp.where(spot < LANES, 2 * spot, 2 * spot - (TILE - 1))
        split = choose(iota((TILE, TILE), 0) == source).astype(BF16)
        keep = choose(iota((1, step), 1) + at * step < length)
        for row in range(0, c_in, LANES):
            count = min(LANES, c_in - row)
            count_pad = up(count, 16)
            pick = choose(
                iota((count_pad, 2 * count), 1) == 2 * iota((count_pad, 2 * count), 0) + section
            ).astype(BF16)
            chosen = nn(pick, flat[2 * row : 2 * (row + count)])
            own[row : row + count_pad, :] = (chosen * keep).astype(BF16)
        low = nn(own[:, :TILE], split)
        high = nn(own[:, TILE:], split)
        x_ref[0, 0, :, :LANES] = low[:, :LANES].astype(BF16)
        x_ref[0, 0, :, LANES:] = high[:, :LANES].astype(BF16)
        x_ref[0, 1, :, :LANES] = low[:, LANES:].astype(BF16)
        x_ref[0, 1, :, LANES:] = high[:, LANES:].astype(BF16)
        s_acc[:c_pad, :] += fold(low) + fold(high)
        q_acc[:c_pad, :] += fold(low * low) + fold(high * high)

        @pl.when(at == steps - 1)
        def _():
            lane = iota((1, c_lane), 1)
            count_in = length.astype(F32)
            count_pool = ((length + 1) // 2).astype(F32)
            put_rows(
                st_ref,
                k,
                jnp.where(lane < c_in, as_row(s_acc[...]), count_in),
                jnp.where(lane < c_in, as_row(q_acc[...]), count_pool),
            )

    return call(
        "load_features",
        body,
        (micro, steps),
        [pl.BlockSpec((1, c_in, 2, step), lambda k, j, _: (k, 0, 0, j))],
        [per_lanes((2, c_pad, TILE)), whole((8, c_lane))],
        [shape_of((micro, 2, c_pad, bins // 2), BF16), shape_of((8, c_lane))],
        [pltpu.VMEM((c_pad, step), BF16)] + [pltpu.VMEM((c_lane, LANES), F32)] * 2,
    )


def activate(micro, c_in, taps, pooled):
    c_pad = up(c_in, 16)
    c_lane = up(c_in, LANES)
    extra = up(taps * c_pad, TILE) - taps * c_pad
    stack_rows = (taps + 1) * c_pad + extra

    def body(info, x_ref, sums, table, stack, col_c, col_s, col_h):
        k = pl.program_id(0)
        length = info[1 + k]
        (centre, _, inverse), _, _ = first_rows(sums, k, c_in)
        col_c[...] = column(centre)
        col_s[...] = column(inverse * table[0:1, :])

        @pl.when(k == 0)
        def _():
            col_h[...] = column(table[1:2, :])

        stack[0, (taps + 1) * c_pad :, :] = jnp.zeros((extra, pooled), BF16)
        masks = pool_mask(length, pooled), odd_mask(length, pooled)

        def rows_body(rows, start):
            c, s, h = (wide(r[rows, :], TILE) for r in (col_c, col_s, col_h))
            here = lambda seg: pl.ds(aligned(seg * c_pad + start), 16)
            for half in range(2):
                parts = []
                for lane in range(0, pooled, TILE):
                    lanes = slice(lane, lane + TILE)
                    v = (x_ref[0, half, rows, lanes].astype(F32) - c) * s + h
                    parts.append((gelu(v) * masks[half][:, lanes]).astype(BF16))
                a = jnp.concatenate(parts, axis=1)
                stack[0, here(half), :] = before(a)
                stack[0, here(2 + half), :] = a
                stack[0, here(4 + half), :] = after(a)

        each_rows(c_pad, rows_body, 8)

    return call(
        "activate",
        body,
        (micro,),
        [per_batch((2, c_pad, pooled)), whole((8, c_lane)), whole((8, c_lane))],
        per_batch((stack_rows, pooled)),
        shape_of((micro, stack_rows, pooled), BF16),
        [pltpu.VMEM((c_lane, LANES), F32)] * 3,
    )


def lane_blocks(shape, steps, last, late):
    def place(s, _):
        s = jnp.maximum(s - 1, 0) if late else jnp.minimum(s, last)
        return (s // steps,) + (0,) * (len(shape) - 1) + (s % steps,)

    return pl.BlockSpec((1,) + shape, place)


def forward_first(micro, c_in, c_mid, taps, pooled):
    c_pad = up(c_in, 16)
    c_lane = up(c_in, LANES)
    depth = up(taps * c_pad, TILE)
    steps = pooled // STEP
    total = micro * steps
    stack_rows = c_pad + depth
    room = up(c_pad + (taps - 1) * (c_pad % LANES), LANES)
    base = c_pad - c_pad % LANES

    def body(info, stack, table, weight, hid, diff, st_ref,
             bias, s_acc, q_acc, even, odd, held, line):
        step = pl.program_id(0)
        late = jnp.maximum(step - 1, 0)
        k, at = late // steps, late % steps
        mask = pool_mask(info[1 + k], STEP, at * STEP)

        @pl.when(step == 0)
        def _():
            bias[...] = column(table[2:3, :c_mid])
            st_ref[...] = jnp.zeros_like(st_ref)
            eye = identity()
            for row in range(0, c_mid, TILE):
                line[...] = jnp.zeros_like(line)
                for tap in range(taps):
                    turned = nt(eye, weight[tap, :, row : row + TILE])
                    padded = jnp.concatenate([turned, jnp.zeros((TILE, room - c_in), F32)], axis=1)
                    moved = pltpu.roll(padded, tap * (c_pad % LANES), 1) if tap else padded
                    line[:, tap * base : tap * base + room] += moved
                held[row : row + TILE, :] = line[:, :depth].astype(BF16)

        @pl.when(at == 0)
        def _():
            s_acc[...] = jnp.zeros_like(s_acc)
            q_acc[...] = jnp.zeros_like(q_acc)

        def finish():
            for start in range(0, c_mid, 16):
                rows = slice(start, start + 16)
                b = wide(bias[rows, :], STEP)
                left, right = even[rows, :] + b, odd[rows, :] + b
                apart = left - right
                joined = jnp.maximum(left, right) + jnp.log1p(jnp.exp(-jnp.abs(apart)))
                rounded = (joined * mask).astype(BF16)
                diff[0, rows, :] = apart
                hid[0, rows, :] = rounded
                value = rounded.astype(F32)
                s_acc[rows, :] += fold(value)
                q_acc[rows, :] += fold(value * value)

        @pl.when(step < total)
        def _():
            finish()
            even[...] = nn(held[...], stack[0, :depth, :])
            odd[...] = nn(held[...], stack[0, c_pad : c_pad + depth, :])

        @pl.when(step == total)
        def _():
            finish()

        @pl.when(at == steps - 1)
        def _():
            put_rows(st_ref, k, as_row(s_acc[...]), as_row(q_acc[...]))

    return call(
        "forward_first",
        body,
        (total + 1,),
        [
            lane_blocks((stack_rows, STEP), steps, total - 1, False),
            whole((8, c_lane)),
            whole((taps, c_in, c_mid), 1),
        ],
        [
            lane_blocks((c_mid, STEP), steps, total - 1, True),
            lane_blocks((c_mid, STEP), steps, total - 1, True),
            whole((8, c_mid)),
        ],
        [
            shape_of((micro, c_mid, pooled), BF16),
            shape_of((micro, c_mid, pooled)),
            shape_of((8, c_mid)),
        ],
        [pltpu.VMEM((c_mid, LANES), F32)] * 3
        + [pltpu.VMEM((c_mid, STEP), F32)] * 2
        + [
            pltpu.VMEM((c_mid, depth), BF16),
            pltpu.VMEM((TILE, max(depth, (taps - 1) * base + room)), F32),
        ],
    )


def forward_second(micro, c_in, c_mid, c_res, taps, pooled, c_lane):
    def body(info, hid, sums_a, sums, table, weight, conv, act, st_ref,
             stack, col_c, col_s, col_h, s_acc, q_acc, held):
        k = pl.program_id(0)
        length = info[1 + k]
        _, _, count = first_rows(sums_a, k, c_in)
        centre, _, inverse = finish_rows(row_pair(sums, k), count)
        col_c[...] = column(centre)
        col_s[...] = column(inverse * table[3:4, :c_mid])

        @pl.when(k == 0)
        def _():
            col_h[...] = column(table[4:5, :c_mid])
            st_ref[...] = jnp.zeros_like(st_ref)
            eye = choose(iota((c_res, c_res), 0) == iota((c_res, c_res), 1)).astype(BF16)
            for tap in range(taps):
                held[:, tap * c_mid : (tap + 1) * c_mid] = nt(eye, weight[tap]).astype(BF16)

        mask = pool_mask(length, pooled)

        def rows_body(rows, start):
            c, s, h = (wide(r[rows, :], TILE) for r in (col_c, col_s, col_h))
            here = lambda seg: pl.ds(aligned(seg * c_mid + start), 16)
            parts = []
            for lane in range(0, pooled, TILE):
                lanes = slice(lane, lane + TILE)
                v = (hid[0, rows, lanes].astype(F32) - c) * s + h
                parts.append((gelu(v) * mask[:, lanes]).astype(BF16))
            a = jnp.concatenate(parts, axis=1)
            act[0, rows, :] = a
            stack[here(0), :] = before(a)
            stack[here(1), :] = a
            stack[here(2), :] = after(a)

        each_rows(c_mid, rows_body, 8)
        conv[0] = nn(held[...], stack[...])

        def moments_body(rows, start):
            value = conv[0, rows, :] * mask
            s_acc[rows, :] = fold(value)
            q_acc[rows, :] = fold(value * value)

        each_rows(c_res, moments_body, 8)
        put_rows(st_ref, k, as_row(s_acc[...]), as_row(q_acc[...]))

    return call(
        "forward_second",
        body,
        (micro,),
        [
            per_batch((c_mid, pooled)),
            whole((8, c_lane)),
            whole((8, c_mid)),
            whole((8, c_lane)),
            whole((taps, c_mid, c_res), 1),
        ],
        [per_batch((c_res, pooled)), per_batch((c_mid, pooled)), whole((8, c_res))],
        [
            shape_of((micro, c_res, pooled)),
            shape_of((micro, c_mid, pooled), BF16),
            shape_of((8, c_res)),
        ],
        [pltpu.VMEM((taps * c_mid, pooled), BF16)]
        + [pltpu.VMEM((c_mid, LANES), F32)] * 3
        + [pltpu.VMEM((c_res, LANES), F32)] * 2
        + [pltpu.VMEM((c_res, taps * c_mid), BF16)],
        after=1,
    )


def turn_cotangent(micro, c_mid, c_res, pooled):
    def body(info, cot, point, go, up_grad, grad_bias):
        k = pl.program_id(0)
        mask = pool_mask(info[1 + k], pooled)
        eye = identity()
        up_grad[0] = nt(point[...], cot[0, 0])
        for at in range(0, c_mid, TILE):
            go[0, at : at + TILE, :] = (nt(eye, cot[0, 0, :, at : at + TILE]) * mask).astype(BF16)
        ones = jnp.broadcast_to(mask, (16, pooled)).astype(BF16)
        total = nn(ones, cot[0, 0])[:8]
        grad_bias[...] = total + jnp.where(k == 0, 0.0, grad_bias[...])

    return call(
        "turn_cotangent",
        body,
        (micro,),
        [
            pl.BlockSpec((1, 1, pooled, c_mid), lambda k, info: (k, info[0], 0, 0)),
            whole((c_res, c_mid), 1),
        ],
        [per_batch((c_mid, pooled)), per_batch((c_res, pooled)), whole((8, c_mid))],
        [
            shape_of((micro, c_mid, pooled), BF16),
            shape_of((micro, c_res, pooled)),
            shape_of((8, c_mid)),
        ],
    )


def norm_third(micro, c_in, c_res, pooled, c_lane):
    def body(info, conv, up_grad, sums_a, sums, table, act, d_out, st_ref,
             col_c, col_s, col_h, s_acc, q_acc):
        k = pl.program_id(0)
        length = info[1 + k]
        _, _, count = first_rows(sums_a, k, c_in)
        centre, _, inverse = finish_rows(row_pair(sums, k), count)
        col_c[...] = column(centre)
        col_s[...] = column(inverse * table[5:6, :c_res])

        @pl.when(k == 0)
        def _():
            col_h[...] = column(table[6:7, :c_res])
            st_ref[...] = jnp.zeros_like(st_ref)

        mask = pool_mask(length, pooled)

        def rows_body(rows, start):
            c, s, h = (wide(r[rows, :], TILE) for r in (col_c, col_s, col_h))
            total_s, total_q = [], []
            for lane in range(0, pooled, TILE):
                lanes = slice(lane, lane + TILE)
                apart = conv[0, rows, lanes] - c
                a, slope = gelu_slope(apart * s + h)
                act[0, rows, lanes] = (a * mask[:, lanes]).astype(BF16)
                d = mask[:, lanes] * slope * up_grad[0, rows, lanes]
                d_out[0, rows, lanes] = d
                total_s.append(fold(d))
                total_q.append(fold(d * apart))
            s_acc[rows, :] = sum(total_s)
            q_acc[rows, :] = sum(total_q)

        each_rows(c_res, rows_body, 8)
        put_rows(st_ref, k, as_row(s_acc[...]), as_row(q_acc[...]) * inverse)

    return call(
        "norm_third",
        body,
        (micro,),
        [
            per_batch((c_res, pooled)),
            per_batch((c_res, pooled)),
            whole((8, c_lane)),
            whole((8, c_res)),
            whole((8, c_lane)),
        ],
        [per_batch((c_res, pooled)), per_batch((c_res, pooled)), whole((8, c_res))],
        [
            shape_of((micro, c_res, pooled), BF16),
            shape_of((micro, c_res, pooled)),
            shape_of((8, c_res)),
        ],
        [pltpu.VMEM((c_res, LANES), F32)] * 5,
    )


def point_output(micro, c_mid, c_res, pooled, c_lane):
    half = c_mid // 2

    def body(info, act, hid, table, point, own, send, branch, flat, bias, held):
        k = pl.program_id(0)
        first = info[0] == 0
        mask = pool_mask(info[1 + k], pooled)

        @pl.when(k == 0)
        def _():
            bias[...] = column(table[7:8, :c_mid])
            eye = choose(iota((c_mid, c_mid), 0) == iota((c_mid, c_mid), 1)).astype(BF16)
            held[...] = nt(eye, point[...]).astype(BF16)

        branch[...] = nn(held[...], act[0])

        def out_body(rows, start):
            b = wide(bias[rows, :], pooled)
            value = hid[0, rows, :].astype(F32) + (branch[rows, :] + b)
            flat[rows, :] = (value * mask).astype(BF16)

        each_rows(c_mid, out_body, 8)
        eye = identity()
        for at in range(0, pooled, TILE):
            turned = nt(eye, flat[:, at : at + TILE]).astype(BF16)
            low, high = turned[:, :half], turned[:, half:]
            own[0, at : at + TILE, :] = jnp.where(first, low, high)
            send[0, at : at + TILE, :] = jnp.where(first, high, low)

    return call(
        "point_output",
        body,
        (micro,),
        [
            per_batch((c_res, pooled)),
            per_batch((c_mid, pooled)),
            whole((8, c_lane)),
            whole((c_res, c_mid), 1),
        ],
        [per_batch((pooled, half)), per_batch((pooled, half))],
        [
            shape_of((micro, pooled, half), BF16),
            shape_of((micro, pooled, half), BF16),
        ],
        [
            pltpu.VMEM((c_mid, pooled), F32),
            pltpu.VMEM((c_mid, pooled), BF16),
            pltpu.VMEM((c_mid, LANES), F32),
            pltpu.VMEM((c_mid, c_res), BF16),
        ],
    )


def backward_second(micro, c_in, c_mid, c_res, taps, pooled, c_lane):
    def body(info, d_in, conv, sums_a, sums_b, sums_c, back, table, hid, weight,
             d_out, st_ref, stack,
             up_grad, col_a, col_b, col_0, col_r, col_c, col_s, col_h, s_acc, q_acc, held, kept):
        k = pl.program_id(0)
        length = info[1 + k]
        _, _, count = first_rows(sums_a, k, c_in)
        centre, _, inverse = finish_rows(row_pair(sums_c, k), count)
        outer, slant, level = back_rows(row_pair(back, k), count, table[5:6, :c_res], inverse)
        col_a[...] = column(outer)
        col_b[...] = column(slant)
        col_0[...] = column(level)
        col_r[...] = column(centre)
        centre, _, inverse = finish_rows(row_pair(sums_b, k), count)
        col_c[...] = column(centre)
        col_s[...] = column(inverse * table[3:4, :c_mid])

        @pl.when(k == 0)
        def _():
            col_h[...] = column(table[4:5, :c_mid])
            st_ref[...] = jnp.zeros_like(st_ref)
            for tap in range(taps):
                held[:, tap * c_res : (tap + 1) * c_res] = weight[tap]

        mask = pool_mask(length, pooled)

        def rows_body(rows, start):
            a, b, z, c = (wide(r[rows, :], pooled) for r in (col_a, col_b, col_0, col_r))
            g = (a * d_in[0, rows, :] - b * (conv[0, rows, :] - c) - z) * mask
            g = g.astype(BF16)
            here = lambda seg: pl.ds(aligned(seg * c_res + start), 16)
            for order, value in enumerate((after(g), g, before(g))):
                stack[0, here(order), :] = value
                kept[here(order), :] = value

        each_rows(c_res, rows_body, 8)
        up_grad[...] = nn(held[...], kept[...])

        def slope_body(rows, start):
            c, s, h = (wide(r[rows, :], TILE) for r in (col_c, col_s, col_h))
            total_s, total_q = [], []
            for lane in range(0, pooled, TILE):
                lanes = slice(lane, lane + TILE)
                apart = hid[0, rows, lanes].astype(F32) - c
                _, slope = gelu_slope(apart * s + h)
                d = mask[:, lanes] * slope * up_grad[rows, lanes]
                d_out[0, rows, lanes] = d
                total_s.append(fold(d))
                total_q.append(fold(d * apart))
            s_acc[rows, :] = sum(total_s)
            q_acc[rows, :] = sum(total_q)

        each_rows(c_mid, slope_body, 8)
        put_rows(st_ref, k, as_row(s_acc[...]), as_row(q_acc[...]) * inverse)

    in_specs = [
        per_batch((c_res, pooled)),
        per_batch((c_res, pooled)),
        whole((8, c_lane)),
        whole((8, c_mid)),
        whole((8, c_res)),
        whole((8, c_res)),
        whole((8, c_lane)),
        per_batch((c_mid, pooled)),
        whole((taps, c_mid, c_res), 1),
    ]
    return call(
        "backward_second",
        body,
        (micro,),
        in_specs,
        [per_batch((c_mid, pooled)), whole((8, c_mid)), per_batch((taps * c_res, pooled))],
        [
            shape_of((micro, c_mid, pooled)),
            shape_of((8, c_mid)),
            shape_of((micro, taps * c_res, pooled), BF16),
        ],
        [pltpu.VMEM((c_mid, pooled), F32)]
        + [pltpu.VMEM((c_res, LANES), F32)] * 4
        + [pltpu.VMEM((c_mid, LANES), F32)] * 5
        + [pltpu.VMEM((c_mid, taps * c_res), BF16), pltpu.VMEM((taps * c_res, pooled), BF16)],
    )


def weights_second(micro, c_mid, c_res, taps, pooled):
    rows = taps * c_res

    def body(info, act, stack, go, act_c, grad_conv, grad_point, product, product_point):
        k = pl.program_id(0)
        product[...] = nt(stack[0], act[0]) + jnp.where(k == 0, 0.0, product[...])
        product_point[...] = nt(act_c[0], go[0]) + jnp.where(k == 0, 0.0, product_point[...])

        @pl.when(k == micro - 1)
        def _():
            grad_point[...] = product_point[...].astype(BF16)
            eye = identity()
            for tap in range(taps):
                block = product[tap * c_res : (tap + 1) * c_res, :].astype(BF16)
                for row in range(0, c_mid, TILE):
                    turned = nt(eye, block[:, row : row + TILE])
                    grad_conv[tap, row : row + TILE, :] = turned.astype(BF16)

    return call(
        "weights_second",
        body,
        (micro,),
        [
            per_batch((c_mid, pooled)),
            per_batch((rows, pooled)),
            per_batch((c_mid, pooled)),
            per_batch((c_res, pooled)),
        ],
        [whole((taps, c_mid, c_res)), whole((c_res, c_mid))],
        [shape_of((taps, c_mid, c_res), BF16), shape_of((c_res, c_mid), BF16)],
        [pltpu.VMEM((rows, c_mid), F32), pltpu.VMEM((c_res, c_mid), F32)],
    )


def gradient_first(micro, c_in, c_mid, taps, pooled, c_lane):
    def body(info, d_in, hid, go, diff, sums_a, sums_b, back, table,
             g_out, bias_out, col_a, col_b, col_0, col_c, s_acc):
        k = pl.program_id(0)
        length = info[1 + k]
        _, _, count = first_rows(sums_a, k, c_in)
        centre, _, inverse = finish_rows(row_pair(sums_b, k), count)
        outer, slant, level = back_rows(row_pair(back, k), count, table[3:4, :c_mid], inverse)
        col_a[...] = column(outer)
        col_b[...] = column(slant)
        col_0[...] = column(level)
        col_c[...] = column(centre)
        mask = pool_mask(length, pooled)

        def rows_body(rows, start):
            a, b, z, c = (wide(r[rows, :], TILE) for r in (col_a, col_b, col_0, col_c))
            lefts, rights, totals = [], [], []
            for lane in range(0, pooled, TILE):
                lanes = slice(lane, lane + TILE)
                field = a * d_in[0, rows, lanes] - b * (hid[0, rows, lanes].astype(F32) - c) - z
                g = field * mask[:, lanes] + go[0, rows, lanes].astype(F32)
                g = g.astype(BF16).astype(F32)
                apart = diff[0, rows, lanes]
                small = jnp.exp(-jnp.abs(apart))
                large = 1.0 / (1.0 + small)
                small = small * large
                positive = apart >= 0.0
                left = (g * jnp.where(positive, large, small)).astype(BF16)
                right = (g * jnp.where(positive, small, large)).astype(BF16)
                lefts.append(left)
                rights.append(right)
                totals.append(fold(left.astype(F32) + right.astype(F32)))
            s_acc[rows, :] = sum(totals)
            for side, parts in enumerate((lefts, rights)):
                g_out[0, side, rows, :] = jnp.concatenate(parts, axis=1)

        each_rows(c_mid, rows_body, 6)
        bias_out[...] = as_row(s_acc[...]) + jnp.where(k == 0, 0.0, bias_out[...])

    in_specs = [
        per_batch((c_mid, pooled)),
        per_batch((c_mid, pooled)),
        per_batch((c_mid, pooled)),
        per_batch((c_mid, pooled)),
        whole((8, c_lane)),
        whole((8, c_mid)),
        whole((8, c_mid)),
        whole((8, c_lane)),
    ]
    return call(
        "gradient_first",
        body,
        (micro,),
        in_specs,
        [per_batch((2, c_mid, pooled)), whole((8, c_mid))],
        [shape_of((micro, 2, c_mid, pooled), BF16), shape_of((8, c_mid))],
        [pltpu.VMEM((c_mid, LANES), F32)] * 5,
        after=1,
    )


def weights_first(micro, c_in, c_mid, taps, pooled):
    c_pad = up(c_in, 16)

    def body(info, act_left, act_right, left, right, grad_conv, product, held_left, held_right):
        k, at = pl.program_id(0), pl.program_id(1)

        @pl.when(at == 0)
        def _():
            held_left[...] = left[0, 0]
            held_right[...] = right[0, 0]

        value = nt(act_left[0], held_left[...]) + nt(act_right[0], held_right[...])
        product[at] = value + jnp.where(k == 0, 0.0, product[at])

        @pl.when(k == micro - 1)
        def _():
            grad_conv[0] = product[at, :c_in, :].astype(BF16)

    def act_block(shift):
        return pl.BlockSpec((1, c_pad, pooled), lambda k, j, _: (k, j + shift, 0))

    def grad_block(side):
        return pl.BlockSpec((1, 1, c_mid, pooled), lambda k, j, _: (k, side, 0, 0))

    return call(
        "weights_first",
        body,
        (micro, taps),
        [act_block(0), act_block(1), grad_block(0), grad_block(1)],
        pl.BlockSpec(
            (1, c_in, c_mid), lambda k, j, _: (jnp.where(k == micro - 1, j, 0), 0, 0)
        ),
        shape_of((taps, c_in, c_mid), BF16),
        [pltpu.VMEM((taps, c_pad, c_mid), F32)] + [pltpu.VMEM((c_mid, pooled), BF16)] * 2,
        after=1,
    )


def backward_first(micro, c_in, c_mid, taps, pooled, c_lane):
    c_pad = up(c_in, 16)
    steps = pooled // STEP
    total = micro * steps
    depth = taps * c_mid

    def body(info, g_in, x_ref, sums_a, table, weight, bias_first, bias_point, d_out, st_ref,
             even, odd, col_c, col_s, col_h, s_acc, q_acc, held, stack):
        step = pl.program_id(0)
        late = jnp.maximum(step - 1, 0)
        k, at = late // steps, late % steps
        length = info[1 + k]
        (centre, _, inverse), _, _ = first_rows(sums_a, k, c_in)
        masks = pool_mask(length, STEP, at * STEP), odd_mask(length, STEP, at * STEP)

        @pl.when(step == 0)
        def _():
            col_h[...] = column(table[1:2, :])
            st_ref[...] = jnp.zeros_like(st_ref)
            held[c_in:, :] = jnp.zeros((c_pad - c_in, depth), BF16)
            for tap in range(taps):
                held[:c_in, tap * c_mid : (tap + 1) * c_mid] = weight[tap]
            st_ref[2 * micro : 2 * micro + 1, :] = bias_first[0:1, :]
            st_ref[2 * micro + 1 : 2 * micro + 2, :] = bias_point[0:1, :]

        @pl.when(at == 0)
        def _():
            col_c[...] = column(centre)
            col_s[...] = column(inverse * table[0:1, :])
            s_acc[...] = jnp.zeros_like(s_acc)
            q_acc[...] = jnp.zeros_like(q_acc)

        @pl.when((step % steps == 0) & (step < total))
        def _():
            def rows_body(rows, start):
                here = lambda seg: pl.ds(aligned(seg * c_mid + start), 16)
                for side in range(2):
                    value = g_in[0, side, rows, :]
                    order = 3 - side
                    stack[here(order - 2), :] = after(value)
                    stack[here(order), :] = value
                    stack[here(order + 2), :] = before(value)

            each_rows(c_mid, rows_body, 8)

        lanes = pl.ds(pl.multiple_of((step % steps) * STEP, STEP), STEP)

        def finish():
            for start in range(0, c_pad, 16):
                rows = slice(start, start + 16)
                c, s, h = (wide(r[rows, :], STEP) for r in (col_c, col_s, col_h))
                for half, upstream in enumerate((even, odd)):
                    apart = x_ref[0, half, rows, :].astype(F32) - c
                    _, slope = gelu_slope(apart * s + h)
                    d = masks[half] * slope * upstream[rows, :]
                    d_out[0, half, rows, :] = d
                    s_acc[rows, :] += fold(d)
                    q_acc[rows, :] += fold(d * apart)

        @pl.when(step < total)
        def _():
            finish()
            even[...] = nn(held[...], stack[c_mid : c_mid + depth, lanes])
            odd[...] = nn(held[...], stack[:depth, lanes])

        @pl.when(step == total)
        def _():
            finish()

        @pl.when(at == steps - 1)
        def _():
            put_rows(st_ref, k, as_row(s_acc[...]), as_row(q_acc[...]) * inverse)

    return call(
        "backward_first",
        body,
        (total + 1,),
        [
            pl.BlockSpec(
                (1, 2, c_mid, pooled),
                lambda s, _: (jnp.minimum(s, total - 1) // steps, 0, 0, 0),
            ),
            lane_blocks((2, c_pad, STEP), steps, total - 1, True),
            whole((8, c_lane)),
            whole((8, c_lane)),
            whole((taps, c_in, c_mid), 1),
            whole((8, c_mid)),
            whole((8, c_mid)),
        ],
        [lane_blocks((2, c_pad, STEP), steps, total - 1, True), whole((8, c_lane))],
        [shape_of((micro, 2, c_pad, pooled)), shape_of((8, c_lane))],
        [pltpu.VMEM((c_pad, STEP), F32)] * 2
        + [pltpu.VMEM((c_lane, LANES), F32)] * 5
        + [pltpu.VMEM((c_pad, depth), BF16), pltpu.VMEM((depth + c_mid, pooled), BF16)],
    )


def finish_first(micro, c_in, pooled, c_lane):
    c_pad = up(c_in, 16)
    half_in = c_in // 2
    steps = pooled // TILE

    def body(info, d_in, x_ref, sums_a, back, table, own, send, flat, col_a, col_b, col_0, col_c):
        k, at = pl.program_id(0), pl.program_id(1)
        section, length = info[0], info[1 + k]

        @pl.when(at == 0)
        def _():
            (centre, _, inverse), count, _ = first_rows(sums_a, k, c_in)
            outer, slant, level = back_rows(row_pair(back, k), count, table[0:1, :], inverse)
            col_a[...] = column(outer)
            col_b[...] = column(slant)
            col_0[...] = column(level)
            col_c[...] = column(centre)

        masks = pool_mask(length, TILE, at * TILE), odd_mask(length, TILE, at * TILE)

        def rows_body(rows, start):
            a, b, z, c = (wide(r[rows, :], TILE) for r in (col_a, col_b, col_0, col_c))
            parts = []
            for half in range(2):
                apart = x_ref[0, half, rows, :].astype(F32) - c
                field = (a * d_in[0, half, rows, :] - b * apart - z) * masks[half]
                parts.append(field.astype(BF16))
            for side in range(0, TILE, LANES):
                flat[rows, 2 * side : 2 * side + LANES] = parts[0][:, side : side + LANES]
                flat[rows, 2 * side + LANES : 2 * side + TILE] = parts[1][:, side : side + LANES]

        each_rows(c_pad, rows_body, 10)
        spot = iota((TILE, TILE), 0)
        source = jnp.where(spot < LANES, 2 * spot, 2 * spot - (TILE - 1))
        join = choose(iota((TILE, TILE), 1) == source).astype(BF16)
        for side in range(0, 2 * TILE, TILE):
            natural = nn(flat[:, side : side + TILE], join)
            low, high = natural[:half_in], natural[half_in : 2 * half_in]
            first = section == 0
            own[0, :, side : side + TILE] = jnp.where(first, low, high).astype(BF16)
            send[0, :, side : side + TILE] = jnp.where(first, high, low).astype(BF16)

    half_block = pl.BlockSpec((1, half_in, 2 * TILE), lambda k, j, _: (k, 0, j))
    return call(
        "finish_first",
        body,
        (micro, steps),
        [
            per_lanes((2, c_pad, TILE)),
            per_lanes((2, c_pad, TILE)),
            whole((8, c_lane)),
            whole((8, c_lane)),
            whole((8, c_lane)),
        ],
        [half_block, half_block],
        [shape_of((micro, half_in, 2 * pooled), BF16)] * 2,
        [pltpu.VMEM((c_pad, 2 * TILE), BF16)] + [pltpu.VMEM((c_lane, LANES), F32)] * 4,
    )


def pair_windows(micro, half_in, bins):
    step = 2 * TILE
    steps = bins // step

    def body(info, own, got, out):
        section = info[0]
        for row in range(0, half_in, LANES):
            count = min(LANES, half_in - row)
            at = iota((2 * count, count), 0) - 2 * iota((2 * count, count), 1)
            joined = nn(choose(at == section).astype(BF16), own[0, row : row + count, :])
            joined += nn(choose(at == 1 - section).astype(BF16), got[0, row : row + count, :])
            out[0, row : row + count] = joined.astype(BF16).reshape(count, 2, step)

    block = pl.BlockSpec((1, half_in, step), lambda k, j, _: (k, 0, j))
    return call(
        "pair_windows",
        body,
        (micro, steps),
        [block, block],
        pl.BlockSpec((1, half_in, 2, step), lambda k, j, _: (k, 0, 0, j)),
        shape_of((micro, half_in, 2, bins), BF16),
    )


def small_outputs(micro, c_in, c_mid, c_res, c_lane):
    def body(info, sums_a, sums_b, sums_c, back_a, back_b, back_c, *rest):
        running = rest[:6]
        outs = rest[6:]

        def put(ref, row):
            ref[...] = row.reshape(row.shape[1])[: ref.shape[0]]

        for at, back in enumerate((back_a, back_b, back_c)):
            put(outs[2 * at], sum(back[2 * k + 1 : 2 * k + 2, :] for k in range(micro)))
            put(outs[2 * at + 1], sum(back[2 * k : 2 * k + 1, :] for k in range(micro)))
        put(outs[6], back_a[2 * micro : 2 * micro + 1, :c_mid])
        put(outs[7], back_a[2 * micro + 1 : 2 * micro + 2, :c_mid])
        firsts = [first_rows(sums_a, k, c_in) for k in range(micro)]
        stats = [[f[0] for f in firsts]]
        for sums in (sums_b, sums_c):
            stats.append(
                [finish_rows(sums[2 * k : 2 * k + 2, :], firsts[k][2]) for k in range(micro)]
            )
        for at, history in enumerate(stats):
            for part in range(2):
                lanes = history[0][part].shape[1]
                value = running[2 * at + part][...]
                if value.shape[0] < lanes:
                    value = jnp.pad(value, (0, lanes - value.shape[0]))
                value = value.reshape(1, lanes)
                for k in range(micro):
                    value = (1.0 - MOMENTUM) * value + MOMENTUM * history[k][part]
                put(outs[8 + 2 * at + part], value)

    widths = [c_in] * 2 + [c_mid] * 2 + [c_res] * 2
    shapes = widths + [c_mid, c_mid] + widths
    tables = [(8, c_lane), (8, c_mid), (8, c_res)] * 2
    return call(
        "small_outputs",
        body,
        (1,),
        [whole(s) for s in tables] + [whole((n,)) for n in widths],
        [whole((n,)) for n in shapes],
        [shape_of((n,)) for n in shapes],
    )


def partner(array):
    return lax.ppermute(array, "section", [(0, 1), (1, 0)])


def share(rows):
    devices = lax.axis_size("section") * lax.axis_size("dp")
    bits = [1 << at for at in range(devices.bit_length() - 1)]
    groups = [[bits[-1], bits[0]]]
    rest = bits[1:-1]
    while rest:
        groups.append(rest[:2])
        rest = rest[2:]
    for group in groups:
        masks = [0]
        for bit in group:
            masks += [mask + bit for mask in masks]
        parts = [
            lax.ppermute(rows, BOTH, [(i, i ^ mask) for i in range(devices)]) if mask else rows
            for mask in masks
        ]
        while len(parts) > 1:
            parts = [a + b for a, b in zip(parts[::2], parts[1::2])]
        rows = parts[0]
    return rows


def shards(
    features,
    lengths,
    gain_first,
    shift_first,
    conv_first,
    bias_first,
    gain_second,
    shift_second,
    conv_second,
    gain_third,
    shift_third,
    conv_point,
    bias_point,
    mean_first,
    variance_first,
    mean_second,
    variance_second,
    mean_third,
    variance_third,
    cotangent,
):
    micro, _, bins, c_in = features.shape
    pooled = bins // 2
    taps, _, c_mid = conv_first.shape
    taps_b, _, c_res = conv_second.shape
    c_lane = up(c_in, LANES)
    section = lax.axis_index("section").astype(jnp.int32)
    lead = section == 0
    own_lengths = jnp.where(lead, lengths[:, 0], lengths[:, 1]).astype(jnp.int32)
    info = jnp.concatenate([section[None], own_lengths])
    feats = features.transpose(0, 3, 1, 2)

    loaded, part = load_features(micro, bins, c_in)(info, feats)
    sums_a = share(part)
    vectors = (
        gain_first, shift_first, bias_first, gain_second, shift_second, gain_third, shift_third,
        bias_point,
    )
    table = prepare_table(vectors, c_lane)(info, *vectors)
    act_a = activate(micro, c_in, taps, pooled)(info, loaded, sums_a, table)
    hid, diff, part = forward_first(micro, c_in, c_mid, taps, pooled)(info, act_a, table, conv_first)
    sums_b = share(part)
    go, up_c, grad_bias = turn_cotangent(micro, c_mid, c_res, pooled)(info, cotangent, conv_point)
    conv_b, act_b, part = forward_second(micro, c_in, c_mid, c_res, taps_b, pooled, c_lane)(
        info, hid, sums_a, sums_b, table, conv_second, grad_bias
    )
    sums_c = share(part)
    act_c, d_c, part = norm_third(micro, c_in, c_res, pooled, c_lane)(
        info, conv_b, up_c, sums_a, sums_c, table
    )
    back_c = share(part)
    d_b, part, stack_b = backward_second(micro, c_in, c_mid, c_res, taps_b, pooled, c_lane)(
        info, d_c, conv_b, sums_a, sums_b, sums_c, back_c, table, hid, conv_second
    )
    back_b = share(part)
    grad_second, grad_point = weights_second(micro, c_mid, c_res, taps_b, pooled)(
        info, act_b, stack_b, go, act_c
    )
    g_a, bias_sum = gradient_first(micro, c_in, c_mid, taps, pooled, c_lane)(
        info, d_b, hid, go, diff, sums_a, sums_b, back_b, table, grad_second
    )
    grad_first = weights_first(micro, c_in, c_mid, taps, pooled)(
        info, act_a, act_a, g_a, g_a, bias_sum
    )
    sums = lax.psum((grad_first, grad_second, grad_point), BOTH)
    running = (
        mean_first, variance_first, mean_second, variance_second, mean_third, variance_third,
    )

    def behind(_):
        d_a, part = backward_first(micro, c_in, c_mid, taps, pooled, c_lane)(
            info, g_a, loaded, sums_a, table, conv_first, bias_sum, grad_bias
        )
        back_a = share(part)
        own_out, send_out = point_output(micro, c_mid, c_res, pooled, c_lane)(
            info, act_c, hid, table, conv_point
        )
        got_out = partner(send_out)
        own_in, send_in = finish_first(micro, c_in, pooled, c_lane)(
            info, d_a, loaded, sums_a, back_a, table
        )
        got_in = partner(send_in)
        small = small_outputs(micro, c_in, c_mid, c_res, c_lane)(
            info, sums_a, sums_b, sums_c, back_a, back_b, back_c, *running
        )
        paired = pair_windows(micro, c_in // 2, bins)(info, own_in, got_in)
        block_output = jnp.stack(
            [jnp.where(lead, own_out, got_out), jnp.where(lead, got_out, own_out)], axis=1
        )
        return paired, block_output, tuple(small)

    def nothing(_):
        shapes = jax.eval_shape(behind, 0)
        return jax.tree.map(lambda s: jnp.zeros(s.shape, s.dtype), shapes)

    paired, block_output, small = lax.cond(info[1] > 0, behind, nothing, 0)
    input_grad = paired.transpose(0, 2, 3, 1)
    sum_first, sum_second, sum_point = (value.astype(F32) for value in sums)
    return (
        block_output,
        input_grad,
        small[0],
        small[1],
        sum_first,
        small[6],
        small[2],
        small[3],
        sum_second,
        small[4],
        small[5],
        sum_point,
        small[7],
        *small[8:],
    )


def solution(mesh):
    wide_spec = P(None, "dp", None, None)
    split_spec = P(None, "dp", None, "section")
    return jax.shard_map(
        shards,
        mesh=mesh,
        in_specs=(wide_spec, P(None, "dp")) + (P(),) * 17 + (wide_spec,),
        out_specs=(split_spec, split_spec) + (P(),) * 17,
        check_vma=False,
    )
```

```python
from math import pi, sqrt

import jax
import jax.numpy as jnp
from jax import lax
from jax.experimental import pallas as pl
from jax.experimental.pallas import tpu as pltpu
from jax.sharding import PartitionSpec as P

EPSILON = 1e-05
MOMENTUM = 0.4
CURVE = sqrt(2.0 / pi)
CUBIC = CURVE * 0.044715
BF16 = jnp.bfloat16
F32 = jnp.float32
LANES = 128
TILE = 256
STEP = 512
BOTH = ("section", "dp")


def up(value, step):
    return -(-value // step) * step


def nn(left, right):
    return jnp.dot(left, right, preferred_element_type=F32)


def nt(left, right):
    return lax.dot_general(left, right, (((1,), (1,)), ((), ())), preferred_element_type=F32)


def iota(shape, axis):
    return lax.broadcasted_iota(jnp.int32, shape, axis)


def choose(flag):
    return jnp.where(flag, 1.0, 0.0)


def identity():
    return choose(iota((TILE, TILE), 0) == iota((TILE, TILE), 1)).astype(BF16)


def gelu(v):
    half = 0.5 * v
    return half + half * jnp.tanh(v * (CURVE + CUBIC * (v * v)))


def gelu_slope(v):
    square = v * v
    bent = jnp.tanh(v * (CURVE + CUBIC * square))
    half = 0.5 * v
    slope = (0.5 + 0.5 * bent) + half * (1.0 - bent * bent) * (CURVE + (3.0 * CUBIC) * square)
    return half + half * bent, slope


def column(row):
    return jnp.transpose(jnp.broadcast_to(row, (LANES, row.shape[1])))


def as_row(partial_sums):
    return jnp.sum(jnp.transpose(partial_sums), axis=0, keepdims=True)


def wide(block, lanes):
    return jnp.concatenate([block] * (lanes // LANES), axis=1)


def fold(block):
    parts = [block[:, at : at + LANES] for at in range(0, block.shape[1], LANES)]
    while len(parts) > 1:
        parts = [a + b for a, b in zip(parts[::2], parts[1::2])]
    return parts[0]


def before(block):
    rolled = pltpu.roll(block, 1, 1)
    inner = choose(iota((block.shape[0], LANES), 1) > 0).astype(block.dtype)
    return jnp.concatenate([rolled[:, :LANES] * inner, rolled[:, LANES:]], axis=1)


def after(block):
    last = block.shape[1] - LANES
    rolled = pltpu.roll(block, block.shape[1] - 1, 1)
    inner = choose(iota((block.shape[0], LANES), 1) < LANES - 1).astype(block.dtype)
    return jnp.concatenate([rolled[:, :last], rolled[:, last:] * inner], axis=1)


def aligned(value):
    return value if isinstance(value, int) else pl.multiple_of(value, 16)


def each_rows(total, body, unroll, step=16):
    group = step * unroll
    full = total // group

    def run(index, carry):
        for turn in range(unroll):
            start = pl.multiple_of(index * group + turn * step, step)
            body(pl.ds(start, step), start)
        return carry

    lax.fori_loop(0, full, run, 0)
    for start in range(full * group, total, step):
        body(pl.ds(start, step), start)


def pool_mask(length, lanes, start=0):
    return choose(2 * (iota((1, lanes), 1) + start) < length)


def odd_mask(length, lanes, start=0):
    return choose(2 * (iota((1, lanes), 1) + start) + 1 < length)


def whole(shape, buffered=None):
    zeros = (0,) * len(shape)
    if buffered is None:
        return pl.BlockSpec(shape, lambda *_: zeros)
    return pl.BlockSpec(shape, lambda *_: zeros, pipeline_mode=pl.Buffered(buffered))


def per_batch(shape):
    return pl.BlockSpec((1,) + shape, lambda k, *_: (k,) + (0,) * len(shape))


def per_lanes(shape):
    return pl.BlockSpec((1,) + shape, lambda k, j, _: (k,) + (0,) * (len(shape) - 1) + (j,))


def shape_of(shape, dtype=F32):
    return jax.ShapeDtypeStruct(shape, dtype)


def call(name, body, grid, in_specs, out_specs, out_shape, scratch=(), limit=58, after=0):

    real = len(in_specs) + 1

    def ordered(*refs):
        body(*refs[:real], *refs[real + after :])

    in_specs = list(in_specs) + [pl.BlockSpec(memory_space=pl.ANY)] * after
    return pl.pallas_call(
        ordered,
        grid_spec=pltpu.PrefetchScalarGridSpec(
            num_scalar_prefetch=1,
            grid=grid,
            in_specs=in_specs,
            out_specs=out_specs,
            scratch_shapes=list(scratch),
        ),
        out_shape=out_shape,
        compiler_params=pltpu.CompilerParams(vmem_limit_bytes=limit * 2**20),
        name=name,
    )


def row_pair(ref, k):
    table = ref[...]
    at = iota(table.shape, 0) - 2 * k
    rows = [jnp.sum(jnp.where(at == r, table, 0.0), axis=0, keepdims=True) for r in range(2)]
    return jnp.concatenate(rows, axis=0)


def put_rows(ref, k, first, second):
    table = ref[...]
    at = iota(table.shape, 0) - 2 * k
    ref[...] = jnp.where(at == 0, first, jnp.where(at == 1, second, table))


def finish_rows(total, count):
    centre = total[0:1] / count
    variance = total[1:2] / count - centre * centre
    return centre, variance, lax.rsqrt(variance + EPSILON)


def first_rows(ref, k, c_in):
    total = row_pair(ref, k)
    lane = iota((1, total.shape[1]), 1)
    counts = jnp.sum(jnp.where(lane == c_in, total, 0.0), axis=1, keepdims=True)
    total = jnp.where(lane < c_in, total, 0.0)
    return finish_rows(total, counts[0:1]), counts[0:1], counts[1:2]


def back_rows(total, count, gain, inverse):
    outer = gain * inverse
    return outer, outer * inverse * (total[1:2] / count), outer * (total[0:1] / count)


def prepare_table(vectors, c_lane):
    many = len(vectors)

    def body(info, *refs):
        table = refs[many]
        for index, ref in enumerate(refs[:many]):
            value = ref[...]
            if value.shape[0] < c_lane:
                value = jnp.pad(value, (0, c_lane - value.shape[0]))
            table[index : index + 1, :] = value.reshape(1, c_lane)

    return call(
        "prepare_table",
        body,
        (1,),
        [whole(a.shape) for a in vectors],
        whole((up(many, 8), c_lane)),
        shape_of((up(many, 8), c_lane)),
    )


def load_features(micro, bins, c_in):
    c_pad = up(c_in, 16)
    c_lane = up(c_in, LANES)
    step = 2 * TILE
    steps = bins // step

    def body(info, f_ref, x_ref, st_ref, own, s_acc, q_acc):
        k, at = pl.program_id(0), pl.program_id(1)
        section, length = info[0], info[1 + k]

        @pl.when(at == 0)
        def _():
            s_acc[...] = jnp.zeros_like(s_acc)
            q_acc[...] = jnp.zeros_like(q_acc)

        @pl.when((at == 0) & (k == 0))
        def _():
            st_ref[...] = jnp.zeros_like(st_ref)

        flat = f_ref[0].reshape(2 * c_in, step)
        spot = iota((TILE, TILE), 1)
        source = jnp.where(spot < LANES, 2 * spot, 2 * spot - (TILE - 1))
        split = choose(iota((TILE, TILE), 0) == source).astype(BF16)
        keep = choose(iota((1, step), 1) + at * step < length)
        for row in range(0, c_in, LANES):
            count = min(LANES, c_in - row)
            count_pad = up(count, 16)
            pick = choose(
                iota((count_pad, 2 * count), 1) == 2 * iota((count_pad, 2 * count), 0) + section
            ).astype(BF16)
            chosen = nn(pick, flat[2 * row : 2 * (row + count)])
            own[row : row + count_pad, :] = (chosen * keep).astype(BF16)
        low = nn(own[:, :TILE], split)
        high = nn(own[:, TILE:], split)
        x_ref[0, 0, :, :LANES] = low[:, :LANES].astype(BF16)
        x_ref[0, 0, :, LANES:] = high[:, :LANES].astype(BF16)
        x_ref[0, 1, :, :LANES] = low[:, LANES:].astype(BF16)
        x_ref[0, 1, :, LANES:] = high[:, LANES:].astype(BF16)
        s_acc[:c_pad, :] += fold(low) + fold(high)
        q_acc[:c_pad, :] += fold(low * low) + fold(high * high)

        @pl.when(at == steps - 1)
        def _():
            lane = iota((1, c_lane), 1)
            count_in = length.astype(F32)
            count_pool = ((length + 1) // 2).astype(F32)
            put_rows(
                st_ref,
                k,
                jnp.where(lane < c_in, as_row(s_acc[...]), count_in),
                jnp.where(lane < c_in, as_row(q_acc[...]), count_pool),
            )

    return call(
        "load_features",
        body,
        (micro, steps),
        [pl.BlockSpec((1, c_in, 2, step), lambda k, j, _: (k, 0, 0, j))],
        [per_lanes((2, c_pad, TILE)), whole((8, c_lane))],
        [shape_of((micro, 2, c_pad, bins // 2), BF16), shape_of((8, c_lane))],
        [pltpu.VMEM((c_pad, step), BF16)] + [pltpu.VMEM((c_lane, LANES), F32)] * 2,
    )


def activate(micro, c_in, taps, pooled):
    c_pad = up(c_in, 16)
    c_lane = up(c_in, LANES)
    extra = up(taps * c_pad, TILE) - taps * c_pad
    stack_rows = (taps + 1) * c_pad + extra

    def body(info, x_ref, sums, table, stack, col_c, col_s, col_h):
        k = pl.program_id(0)
        length = info[1 + k]
        (centre, _, inverse), _, _ = first_rows(sums, k, c_in)
        col_c[...] = column(centre)
        col_s[...] = column(inverse * table[0:1, :])

        @pl.when(k == 0)
        def _():
            col_h[...] = column(table[1:2, :])

        stack[0, (taps + 1) * c_pad :, :] = jnp.zeros((extra, pooled), BF16)
        masks = pool_mask(length, pooled), odd_mask(length, pooled)

        def rows_body(rows, start):
            c, s, h = (wide(r[rows, :], TILE) for r in (col_c, col_s, col_h))
            here = lambda seg: pl.ds(aligned(seg * c_pad + start), 16)
            for half in range(2):
                parts = []
                for lane in range(0, pooled, TILE):
                    lanes = slice(lane, lane + TILE)
                    v = (x_ref[0, half, rows, lanes].astype(F32) - c) * s + h
                    parts.append((gelu(v) * masks[half][:, lanes]).astype(BF16))
                a = jnp.concatenate(parts, axis=1)
                stack[0, here(half), :] = before(a)
                stack[0, here(2 + half), :] = a
                stack[0, here(4 + half), :] = after(a)

        each_rows(c_pad, rows_body, 8)

    return call(
        "activate",
        body,
        (micro,),
        [per_batch((2, c_pad, pooled)), whole((8, c_lane)), whole((8, c_lane))],
        per_batch((stack_rows, pooled)),
        shape_of((micro, stack_rows, pooled), BF16),
        [pltpu.VMEM((c_lane, LANES), F32)] * 3,
    )


def lane_blocks(shape, steps, last, late):
    def place(s, _):
        s = jnp.maximum(s - 1, 0) if late else jnp.minimum(s, last)
        return (s // steps,) + (0,) * (len(shape) - 1) + (s % steps,)

    return pl.BlockSpec((1,) + shape, place)


def forward_first(micro, c_in, c_mid, taps, pooled):
    c_pad = up(c_in, 16)
    c_lane = up(c_in, LANES)
    depth = up(taps * c_pad, TILE)
    steps = pooled // STEP
    total = micro * steps
    stack_rows = c_pad + depth
    room = up(c_pad + (taps - 1) * (c_pad % LANES), LANES)
    base = c_pad - c_pad % LANES

    def body(info, stack, table, weight, hid, diff, st_ref,
             bias, s_acc, q_acc, even, odd, even_next, odd_next, held, line):
        step = pl.program_id(0)
        late = jnp.maximum(step - 1, 0)
        k, at = late // steps, late % steps
        mask = pool_mask(info[1 + k], STEP, at * STEP)

        @pl.when(step == 0)
        def _():
            bias[...] = column(table[2:3, :c_mid])
            st_ref[...] = jnp.zeros_like(st_ref)
            eye = identity()
            for row in range(0, c_mid, TILE):
                line[...] = jnp.zeros_like(line)
                for tap in range(taps):
                    turned = nt(eye, weight[tap, :, row : row + TILE])
                    padded = jnp.concatenate([turned, jnp.zeros((TILE, room - c_in), F32)], axis=1)
                    moved = pltpu.roll(padded, tap * (c_pad % LANES), 1) if tap else padded
                    line[:, tap * base : tap * base + room] += moved
                held[row : row + TILE, :] = line[:, :depth].astype(BF16)

        @pl.when(at == 0)
        def _():
            s_acc[...] = jnp.zeros_like(s_acc)
            q_acc[...] = jnp.zeros_like(q_acc)

        def finish(old, first, last):
            for start in range(first, last, 16):
                rows = slice(start, start + 16)
                b = wide(bias[rows, :], STEP)
                left, right = old[0][rows, :] + b, old[1][rows, :] + b
                apart = left - right
                joined = jnp.maximum(left, right) + jnp.log1p(jnp.exp(-jnp.abs(apart)))
                rounded = (joined * mask).astype(BF16)
                diff[0, rows, :] = apart
                hid[0, rows, :] = rounded
                value = rounded.astype(F32)
                s_acc[rows, :] += fold(value)
                q_acc[rows, :] += fold(value * value)

        def both(new, old):
            parts = [(side, lane) for side in range(2) for lane in range(0, STEP, TILE)]
            share_of = c_mid // len(parts)
            for part, (side, lane) in enumerate(parts):
                lanes = slice(lane, lane + TILE)
                taken = slice(side * c_pad, side * c_pad + depth)
                new[side][:, lanes] = nn(held[...], stack[0, taken, lanes])
                finish(old, part * share_of, (part + 1) * share_of)

        pairs = (even, odd), (even_next, odd_next)
        for turn in range(2):

            @pl.when((step < total) & (step % 2 == turn))
            def _(turn=turn):
                both(pairs[turn], pairs[1 - turn])

        @pl.when(step == total)
        def _():
            finish(pairs[(total - 1) % 2], 0, c_mid)

        @pl.when(at == steps - 1)
        def _():
            put_rows(st_ref, k, as_row(s_acc[...]), as_row(q_acc[...]))

    return call(
        "forward_first",
        body,
        (total + 1,),
        [
            lane_blocks((stack_rows, STEP), steps, total - 1, False),
            whole((8, c_lane)),
            whole((taps, c_in, c_mid), 1),
        ],
        [
            lane_blocks((c_mid, STEP), steps, total - 1, True),
            lane_blocks((c_mid, STEP), steps, total - 1, True),
            whole((8, c_mid)),
        ],
        [
            shape_of((micro, c_mid, pooled), BF16),
            shape_of((micro, c_mid, pooled)),
            shape_of((8, c_mid)),
        ],
        [pltpu.VMEM((c_mid, LANES), F32)] * 3
        + [pltpu.VMEM((c_mid, STEP), F32)] * 4
        + [
            pltpu.VMEM((c_mid, depth), BF16),
            pltpu.VMEM((TILE, max(depth, (taps - 1) * base + room)), F32),
        ],
    )


def forward_second(micro, c_in, c_mid, c_res, taps, pooled, c_lane):
    def body(info, hid, sums_a, sums, table, weight, conv, act, st_ref,
             stack, col_c, col_s, col_h, s_acc, q_acc, held):
        k = pl.program_id(0)
        length = info[1 + k]
        _, _, count = first_rows(sums_a, k, c_in)
        centre, _, inverse = finish_rows(row_pair(sums, k), count)
        col_c[...] = column(centre)
        col_s[...] = column(inverse * table[3:4, :c_mid])

        @pl.when(k == 0)
        def _():
            col_h[...] = column(table[4:5, :c_mid])
            st_ref[...] = jnp.zeros_like(st_ref)
            eye = choose(iota((c_res, c_res), 0) == iota((c_res, c_res), 1)).astype(BF16)
            for tap in range(taps):
                held[:, tap * c_mid : (tap + 1) * c_mid] = nt(eye, weight[tap]).astype(BF16)

        mask = pool_mask(length, pooled)

        def rows_body(rows, start):
            c, s, h = (wide(r[rows, :], TILE) for r in (col_c, col_s, col_h))
            here = lambda seg: pl.ds(aligned(seg * c_mid + start), 16)
            parts = []
            for lane in range(0, pooled, TILE):
                lanes = slice(lane, lane + TILE)
                v = (hid[0, rows, lanes].astype(F32) - c) * s + h
                parts.append((gelu(v) * mask[:, lanes]).astype(BF16))
            a = jnp.concatenate(parts, axis=1)
            act[0, rows, :] = a
            stack[here(0), :] = before(a)
            stack[here(1), :] = a
            stack[here(2), :] = after(a)

        each_rows(c_mid, rows_body, 8)
        conv[0] = nn(held[...], stack[...])

        def moments_body(rows, start):
            value = conv[0, rows, :] * mask
            s_acc[rows, :] = fold(value)
            q_acc[rows, :] = fold(value * value)

        each_rows(c_res, moments_body, 8)
        put_rows(st_ref, k, as_row(s_acc[...]), as_row(q_acc[...]))

    return call(
        "forward_second",
        body,
        (micro,),
        [
            per_batch((c_mid, pooled)),
            whole((8, c_lane)),
            whole((8, c_mid)),
            whole((8, c_lane)),
            whole((taps, c_mid, c_res), 1),
        ],
        [per_batch((c_res, pooled)), per_batch((c_mid, pooled)), whole((8, c_res))],
        [
            shape_of((micro, c_res, pooled)),
            shape_of((micro, c_mid, pooled), BF16),
            shape_of((8, c_res)),
        ],
        [pltpu.VMEM((taps * c_mid, pooled), BF16)]
        + [pltpu.VMEM((c_mid, LANES), F32)] * 3
        + [pltpu.VMEM((c_res, LANES), F32)] * 2
        + [pltpu.VMEM((c_res, taps * c_mid), BF16)],
        after=1,
    )


def turn_cotangent(micro, c_mid, c_res, pooled):
    def body(info, cot, point, go, up_grad, grad_bias):
        k = pl.program_id(0)
        mask = pool_mask(info[1 + k], pooled)
        eye = identity()
        up_grad[0] = nt(point[...], cot[0, 0])
        for at in range(0, c_mid, TILE):
            go[0, at : at + TILE, :] = (nt(eye, cot[0, 0, :, at : at + TILE]) * mask).astype(BF16)
        ones = jnp.broadcast_to(mask, (16, pooled)).astype(BF16)
        total = nn(ones, cot[0, 0])[:8]
        grad_bias[...] = total + jnp.where(k == 0, 0.0, grad_bias[...])

    return call(
        "turn_cotangent",
        body,
        (micro,),
        [
            pl.BlockSpec((1, 1, pooled, c_mid), lambda k, info: (k, info[0], 0, 0)),
            whole((c_res, c_mid), 1),
        ],
        [per_batch((c_mid, pooled)), per_batch((c_res, pooled)), whole((8, c_mid))],
        [
            shape_of((micro, c_mid, pooled), BF16),
            shape_of((micro, c_res, pooled)),
            shape_of((8, c_mid)),
        ],
    )


def norm_third(micro, c_in, c_res, pooled, c_lane):
    def body(info, conv, up_grad, sums_a, sums, table, act, d_out, st_ref,
             col_c, col_s, col_h, s_acc, q_acc):
        k = pl.program_id(0)
        length = info[1 + k]
        _, _, count = first_rows(sums_a, k, c_in)
        centre, _, inverse = finish_rows(row_pair(sums, k), count)
        col_c[...] = column(centre)
        col_s[...] = column(inverse * table[5:6, :c_res])

        @pl.when(k == 0)
        def _():
            col_h[...] = column(table[6:7, :c_res])
            st_ref[...] = jnp.zeros_like(st_ref)

        mask = pool_mask(length, pooled)

        def rows_body(rows, start):
            c, s, h = (wide(r[rows, :], TILE) for r in (col_c, col_s, col_h))
            total_s, total_q = [], []
            for lane in range(0, pooled, TILE):
                lanes = slice(lane, lane + TILE)
                apart = conv[0, rows, lanes] - c
                a, slope = gelu_slope(apart * s + h)
                act[0, rows, lanes] = (a * mask[:, lanes]).astype(BF16)
                d = mask[:, lanes] * slope * up_grad[0, rows, lanes]
                d_out[0, rows, lanes] = d
                total_s.append(fold(d))
                total_q.append(fold(d * apart))
            s_acc[rows, :] = sum(total_s)
            q_acc[rows, :] = sum(total_q)

        each_rows(c_res, rows_body, 8)
        put_rows(st_ref, k, as_row(s_acc[...]), as_row(q_acc[...]) * inverse)

    return call(
        "norm_third",
        body,
        (micro,),
        [
            per_batch((c_res, pooled)),
            per_batch((c_res, pooled)),
            whole((8, c_lane)),
            whole((8, c_res)),
            whole((8, c_lane)),
        ],
        [per_batch((c_res, pooled)), per_batch((c_res, pooled)), whole((8, c_res))],
        [
            shape_of((micro, c_res, pooled), BF16),
            shape_of((micro, c_res, pooled)),
            shape_of((8, c_res)),
        ],
        [pltpu.VMEM((c_res, LANES), F32)] * 5,
    )


def point_output(micro, c_mid, c_res, pooled, c_lane):
    half = c_mid // 2

    def body(info, act, hid, table, point, own, send, branch, flat, bias, held):
        k = pl.program_id(0)
        first = info[0] == 0
        mask = pool_mask(info[1 + k], pooled)

        @pl.when(k == 0)
        def _():
            bias[...] = column(table[7:8, :c_mid])
            eye = choose(iota((c_mid, c_mid), 0) == iota((c_mid, c_mid), 1)).astype(BF16)
            held[...] = nt(eye, point[...]).astype(BF16)

        branch[...] = nn(held[...], act[0])

        def out_body(rows, start):
            b = wide(bias[rows, :], pooled)
            value = hid[0, rows, :].astype(F32) + (branch[rows, :] + b)
            flat[rows, :] = (value * mask).astype(BF16)

        each_rows(c_mid, out_body, 8)
        eye = identity()
        for at in range(0, pooled, TILE):
            turned = nt(eye, flat[:, at : at + TILE]).astype(BF16)
            low, high = turned[:, :half], turned[:, half:]
            own[0, at : at + TILE, :] = jnp.where(first, low, high)
            send[0, at : at + TILE, :] = jnp.where(first, high, low)

    return call(
        "point_output",
        body,
        (micro,),
        [
            per_batch((c_res, pooled)),
            per_batch((c_mid, pooled)),
            whole((8, c_lane)),
            whole((c_res, c_mid), 1),
        ],
        [per_batch((pooled, half)), per_batch((pooled, half))],
        [
            shape_of((micro, pooled, half), BF16),
            shape_of((micro, pooled, half), BF16),
        ],
        [
            pltpu.VMEM((c_mid, pooled), F32),
            pltpu.VMEM((c_mid, pooled), BF16),
            pltpu.VMEM((c_mid, LANES), F32),
            pltpu.VMEM((c_mid, c_res), BF16),
        ],
    )


def backward_second(micro, c_in, c_mid, c_res, taps, pooled, c_lane):
    def body(info, d_in, conv, sums_a, sums_b, sums_c, back, table, hid, weight,
             d_out, st_ref, stack,
             up_grad, col_a, col_b, col_0, col_r, col_c, col_s, col_h, s_acc, q_acc, held, kept):
        k = pl.program_id(0)
        length = info[1 + k]
        _, _, count = first_rows(sums_a, k, c_in)
        centre, _, inverse = finish_rows(row_pair(sums_c, k), count)
        outer, slant, level = back_rows(row_pair(back, k), count, table[5:6, :c_res], inverse)
        col_a[...] = column(outer)
        col_b[...] = column(slant)
        col_0[...] = column(level)
        col_r[...] = column(centre)
        centre, _, inverse = finish_rows(row_pair(sums_b, k), count)
        col_c[...] = column(centre)
        col_s[...] = column(inverse * table[3:4, :c_mid])

        @pl.when(k == 0)
        def _():
            col_h[...] = column(table[4:5, :c_mid])
            st_ref[...] = jnp.zeros_like(st_ref)
            for tap in range(taps):
                held[:, tap * c_res : (tap + 1) * c_res] = weight[tap]

        mask = pool_mask(length, pooled)

        def rows_body(rows, start):
            a, b, z, c = (wide(r[rows, :], pooled) for r in (col_a, col_b, col_0, col_r))
            g = (a * d_in[0, rows, :] - b * (conv[0, rows, :] - c) - z) * mask
            g = g.astype(BF16)
            here = lambda seg: pl.ds(aligned(seg * c_res + start), 16)
            for order, value in enumerate((after(g), g, before(g))):
                stack[0, here(order), :] = value
                kept[here(order), :] = value

        each_rows(c_res, rows_body, 8)
        up_grad[...] = nn(held[...], kept[...])

        def slope_body(rows, start):
            c, s, h = (wide(r[rows, :], TILE) for r in (col_c, col_s, col_h))
            total_s, total_q = [], []
            for lane in range(0, pooled, TILE):
                lanes = slice(lane, lane + TILE)
                apart = hid[0, rows, lanes].astype(F32) - c
                _, slope = gelu_slope(apart * s + h)
                d = mask[:, lanes] * slope * up_grad[rows, lanes]
                d_out[0, rows, lanes] = d
                total_s.append(fold(d))
                total_q.append(fold(d * apart))
            s_acc[rows, :] = sum(total_s)
            q_acc[rows, :] = sum(total_q)

        each_rows(c_mid, slope_body, 8)
        put_rows(st_ref, k, as_row(s_acc[...]), as_row(q_acc[...]) * inverse)

    in_specs = [
        per_batch((c_res, pooled)),
        per_batch((c_res, pooled)),
        whole((8, c_lane)),
        whole((8, c_mid)),
        whole((8, c_res)),
        whole((8, c_res)),
        whole((8, c_lane)),
        per_batch((c_mid, pooled)),
        whole((taps, c_mid, c_res), 1),
    ]
    return call(
        "backward_second",
        body,
        (micro,),
        in_specs,
        [per_batch((c_mid, pooled)), whole((8, c_mid)), per_batch((taps * c_res, pooled))],
        [
            shape_of((micro, c_mid, pooled)),
            shape_of((8, c_mid)),
            shape_of((micro, taps * c_res, pooled), BF16),
        ],
        [pltpu.VMEM((c_mid, pooled), F32)]
        + [pltpu.VMEM((c_res, LANES), F32)] * 4
        + [pltpu.VMEM((c_mid, LANES), F32)] * 5
        + [pltpu.VMEM((c_mid, taps * c_res), BF16), pltpu.VMEM((taps * c_res, pooled), BF16)],
    )


def weights_second(micro, c_mid, c_res, taps, pooled):
    rows = taps * c_res

    def body(info, act, stack, go, act_c, grad_conv, grad_point, product, product_point):
        k = pl.program_id(0)
        product[...] = nt(stack[0], act[0]) + jnp.where(k == 0, 0.0, product[...])
        product_point[...] = nt(act_c[0], go[0]) + jnp.where(k == 0, 0.0, product_point[...])

        @pl.when(k == micro - 1)
        def _():
            grad_point[...] = product_point[...].astype(BF16)
            eye = identity()
            for tap in range(taps):
                block = product[tap * c_res : (tap + 1) * c_res, :].astype(BF16)
                for row in range(0, c_mid, TILE):
                    turned = nt(eye, block[:, row : row + TILE])
                    grad_conv[tap, row : row + TILE, :] = turned.astype(BF16)

    return call(
        "weights_second",
        body,
        (micro,),
        [
            per_batch((c_mid, pooled)),
            per_batch((rows, pooled)),
            per_batch((c_mid, pooled)),
            per_batch((c_res, pooled)),
        ],
        [whole((taps, c_mid, c_res)), whole((c_res, c_mid))],
        [shape_of((taps, c_mid, c_res), BF16), shape_of((c_res, c_mid), BF16)],
        [pltpu.VMEM((rows, c_mid), F32), pltpu.VMEM((c_res, c_mid), F32)],
    )


def gradient_first(micro, c_in, c_mid, taps, pooled, c_lane):
    def body(info, d_in, hid, go, diff, sums_a, sums_b, back, table,
             g_out, bias_out, col_a, col_b, col_0, col_c, s_acc):
        k = pl.program_id(0)
        length = info[1 + k]
        _, _, count = first_rows(sums_a, k, c_in)
        centre, _, inverse = finish_rows(row_pair(sums_b, k), count)
        outer, slant, level = back_rows(row_pair(back, k), count, table[3:4, :c_mid], inverse)
        col_a[...] = column(outer)
        col_b[...] = column(slant)
        col_0[...] = column(level)
        col_c[...] = column(centre)
        mask = pool_mask(length, pooled)

        def rows_body(rows, start):
            a, b, z, c = (wide(r[rows, :], TILE) for r in (col_a, col_b, col_0, col_c))
            lefts, rights, totals = [], [], []
            for lane in range(0, pooled, TILE):
                lanes = slice(lane, lane + TILE)
                field = a * d_in[0, rows, lanes] - b * (hid[0, rows, lanes].astype(F32) - c) - z
                g = field * mask[:, lanes] + go[0, rows, lanes].astype(F32)
                g = g.astype(BF16).astype(F32)
                apart = diff[0, rows, lanes]
                small = jnp.exp(-jnp.abs(apart))
                large = 1.0 / (1.0 + small)
                small = small * large
                positive = apart >= 0.0
                left = (g * jnp.where(positive, large, small)).astype(BF16)
                right = (g * jnp.where(positive, small, large)).astype(BF16)
                lefts.append(left)
                rights.append(right)
                totals.append(fold(left.astype(F32) + right.astype(F32)))
            s_acc[rows, :] = sum(totals)
            for side, parts in enumerate((lefts, rights)):
                g_out[0, side, rows, :] = jnp.concatenate(parts, axis=1)

        each_rows(c_mid, rows_body, 6)
        bias_out[...] = as_row(s_acc[...]) + jnp.where(k == 0, 0.0, bias_out[...])

    in_specs = [
        per_batch((c_mid, pooled)),
        per_batch((c_mid, pooled)),
        per_batch((c_mid, pooled)),
        per_batch((c_mid, pooled)),
        whole((8, c_lane)),
        whole((8, c_mid)),
        whole((8, c_mid)),
        whole((8, c_lane)),
    ]
    return call(
        "gradient_first",
        body,
        (micro,),
        in_specs,
        [per_batch((2, c_mid, pooled)), whole((8, c_mid))],
        [shape_of((micro, 2, c_mid, pooled), BF16), shape_of((8, c_mid))],
        [pltpu.VMEM((c_mid, LANES), F32)] * 5,
        after=1,
    )


def weights_first(micro, c_in, c_mid, taps, pooled):
    c_pad = up(c_in, 16)
    rows = taps * c_pad
    steps = c_mid // TILE

    def body(info, act, left, right, grad_conv, product):
        k, at = pl.program_id(0), pl.program_id(1)
        value = nt(act[0, :rows, :], left[0, 0]) + nt(act[0, c_pad : c_pad + rows, :], right[0, 0])
        product[at] = value + jnp.where(k == 0, 0.0, product[at])

        @pl.when(k == micro - 1)
        def _():
            for tap in range(taps):
                own = product[at, tap * c_pad : tap * c_pad + c_in, :]
                grad_conv[tap] = own.astype(BF16)

    def grad_block(side):
        return pl.BlockSpec((1, 1, TILE, pooled), lambda k, j, _: (k, side, j, 0))

    return call(
        "weights_first",
        body,
        (micro, steps),
        [
            per_batch((rows + c_pad, pooled)),
            grad_block(0),
            grad_block(1),
        ],
        pl.BlockSpec(
            (taps, c_in, TILE), lambda k, j, _: (0, 0, jnp.where(k == micro - 1, j, 0))
        ),
        shape_of((taps, c_in, c_mid), BF16),
        [pltpu.VMEM((steps, rows, TILE), F32)],
        after=1,
    )


def widen(first, second, third):
    steps = first[0]
    most = second[0] - 1

    def body(info, first_in, second_in, third_in, first_out, second_out, third_out):
        first_out[...] = first_in[...].astype(F32)

        @pl.when(pl.program_id(0) <= most)
        def _():
            second_out[...] = second_in[...].astype(F32)

        @pl.when(pl.program_id(0) == 0)
        def _():
            third_out[...] = third_in[...].astype(F32)

    specs = [
        pl.BlockSpec((1,) + first[1:], lambda i, _: (i, 0, 0)),
        pl.BlockSpec((1,) + second[1:], lambda i, _: (jnp.minimum(i, most), 0, 0)),
        whole(third),
    ]
    return call(
        "widen",
        body,
        (steps,),
        specs,
        specs,
        [shape_of(s) for s in (first, second, third)],
    )


def backward_first(micro, c_in, c_mid, taps, pooled, c_lane):
    c_pad = up(c_in, 16)
    steps = pooled // STEP
    total = micro * steps
    depth = taps * c_mid

    def body(info, g_in, x_ref, sums_a, table, weight, bias_first, bias_point, d_out, st_ref,
             even, odd, col_c, col_s, col_h, s_acc, q_acc, held, stack):
        step = pl.program_id(0)
        late = jnp.maximum(step - 1, 0)
        k, at = late // steps, late % steps
        length = info[1 + k]
        (centre, _, inverse), _, _ = first_rows(sums_a, k, c_in)
        masks = pool_mask(length, STEP, at * STEP), odd_mask(length, STEP, at * STEP)

        @pl.when(step == 0)
        def _():
            col_h[...] = column(table[1:2, :])
            st_ref[...] = jnp.zeros_like(st_ref)
            held[c_in:, :] = jnp.zeros((c_pad - c_in, depth), BF16)
            for tap in range(taps):
                held[:c_in, tap * c_mid : (tap + 1) * c_mid] = weight[tap]
            st_ref[2 * micro : 2 * micro + 1, :] = bias_first[0:1, :]
            st_ref[2 * micro + 1 : 2 * micro + 2, :] = bias_point[0:1, :]

        @pl.when(at == 0)
        def _():
            col_c[...] = column(centre)
            col_s[...] = column(inverse * table[0:1, :])
            s_acc[...] = jnp.zeros_like(s_acc)
            q_acc[...] = jnp.zeros_like(q_acc)

        @pl.when((step % steps == 0) & (step < total))
        def _():
            def rows_body(rows, start):
                here = lambda seg: pl.ds(aligned(seg * c_mid + start), 16)
                for side in range(2):
                    value = g_in[0, side, rows, :]
                    order = 3 - side
                    stack[here(order - 2), :] = after(value)
                    stack[here(order), :] = value
                    stack[here(order + 2), :] = before(value)

            each_rows(c_mid, rows_body, 8)

        lanes = pl.ds(pl.multiple_of((step % steps) * STEP, STEP), STEP)

        def finish():
            for start in range(0, c_pad, 16):
                rows = slice(start, start + 16)
                c, s, h = (wide(r[rows, :], STEP) for r in (col_c, col_s, col_h))
                for half, upstream in enumerate((even, odd)):
                    apart = x_ref[0, half, rows, :].astype(F32) - c
                    _, slope = gelu_slope(apart * s + h)
                    d = masks[half] * slope * upstream[rows, :]
                    d_out[0, half, rows, :] = d
                    s_acc[rows, :] += fold(d)
                    q_acc[rows, :] += fold(d * apart)

        @pl.when(step < total)
        def _():
            finish()
            even[...] = nn(held[...], stack[c_mid : c_mid + depth, lanes])
            odd[...] = nn(held[...], stack[:depth, lanes])

        @pl.when(step == total)
        def _():
            finish()

        @pl.when(at == steps - 1)
        def _():
            put_rows(st_ref, k, as_row(s_acc[...]), as_row(q_acc[...]) * inverse)

    return call(
        "backward_first",
        body,
        (total + 1,),
        [
            pl.BlockSpec(
                (1, 2, c_mid, pooled),
                lambda s, _: (jnp.minimum(s, total - 1) // steps, 0, 0, 0),
            ),
            lane_blocks((2, c_pad, STEP), steps, total - 1, True),
            whole((8, c_lane)),
            whole((8, c_lane)),
            whole((taps, c_in, c_mid), 1),
            whole((8, c_mid)),
            whole((8, c_mid)),
        ],
        [lane_blocks((2, c_pad, STEP), steps, total - 1, True), whole((8, c_lane))],
        [shape_of((micro, 2, c_pad, pooled)), shape_of((8, c_lane))],
        [pltpu.VMEM((c_pad, STEP), F32)] * 2
        + [pltpu.VMEM((c_lane, LANES), F32)] * 5
        + [pltpu.VMEM((c_pad, depth), BF16), pltpu.VMEM((depth + c_mid, pooled), BF16)],
    )


def finish_first(micro, c_in, pooled, c_lane):
    c_pad = up(c_in, 16)
    half_in = c_in // 2
    steps = pooled // TILE

    def body(info, d_in, x_ref, sums_a, back, table, own, send, flat, col_a, col_b, col_0, col_c):
        k, at = pl.program_id(0), pl.program_id(1)
        section, length = info[0], info[1 + k]

        @pl.when(at == 0)
        def _():
            (centre, _, inverse), count, _ = first_rows(sums_a, k, c_in)
            outer, slant, level = back_rows(row_pair(back, k), count, table[0:1, :], inverse)
            col_a[...] = column(outer)
            col_b[...] = column(slant)
            col_0[...] = column(level)
            col_c[...] = column(centre)

        masks = pool_mask(length, TILE, at * TILE), odd_mask(length, TILE, at * TILE)

        def rows_body(rows, start):
            a, b, z, c = (wide(r[rows, :], TILE) for r in (col_a, col_b, col_0, col_c))
            parts = []
            for half in range(2):
                apart = x_ref[0, half, rows, :].astype(F32) - c
                field = (a * d_in[0, half, rows, :] - b * apart - z) * masks[half]
                parts.append(field.astype(BF16))
            for side in range(0, TILE, LANES):
                flat[rows, 2 * side : 2 * side + LANES] = parts[0][:, side : side + LANES]
                flat[rows, 2 * side + LANES : 2 * side + TILE] = parts[1][:, side : side + LANES]

        each_rows(c_pad, rows_body, 10)
        spot = iota((TILE, TILE), 0)
        source = jnp.where(spot < LANES, 2 * spot, 2 * spot - (TILE - 1))
        join = choose(iota((TILE, TILE), 1) == source).astype(BF16)
        for side in range(0, 2 * TILE, TILE):
            natural = nn(flat[:, side : side + TILE], join)
            low, high = natural[:half_in], natural[half_in : 2 * half_in]
            first = section == 0
            own[0, :, side : side + TILE] = jnp.where(first, low, high).astype(BF16)
            send[0, :, side : side + TILE] = jnp.where(first, high, low).astype(BF16)

    half_block = pl.BlockSpec((1, half_in, 2 * TILE), lambda k, j, _: (k, 0, j))
    return call(
        "finish_first",
        body,
        (micro, steps),
        [
            per_lanes((2, c_pad, TILE)),
            per_lanes((2, c_pad, TILE)),
            whole((8, c_lane)),
            whole((8, c_lane)),
            whole((8, c_lane)),
        ],
        [half_block, half_block],
        [shape_of((micro, half_in, 2 * pooled), BF16)] * 2,
        [pltpu.VMEM((c_pad, 2 * TILE), BF16)] + [pltpu.VMEM((c_lane, LANES), F32)] * 4,
    )


def pair_windows(micro, half_in, bins):
    step = 2 * TILE
    steps = bins // step

    def body(info, own, got, out):
        section = info[0]
        for row in range(0, half_in, LANES):
            count = min(LANES, half_in - row)
            at = iota((2 * count, count), 0) - 2 * iota((2 * count, count), 1)
            joined = nn(choose(at == section).astype(BF16), own[0, row : row + count, :])
            joined += nn(choose(at == 1 - section).astype(BF16), got[0, row : row + count, :])
            out[0, row : row + count] = joined.astype(BF16).reshape(count, 2, step)

    block = pl.BlockSpec((1, half_in, step), lambda k, j, _: (k, 0, j))
    return call(
        "pair_windows",
        body,
        (micro, steps),
        [block, block],
        pl.BlockSpec((1, half_in, 2, step), lambda k, j, _: (k, 0, 0, j)),
        shape_of((micro, half_in, 2, bins), BF16),
    )


def small_outputs(micro, c_in, c_mid, c_res, c_lane):
    def body(info, sums_a, sums_b, sums_c, back_a, back_b, back_c, *rest):
        running = rest[:6]
        outs = rest[6:]

        def put(ref, row):
            ref[...] = row.reshape(row.shape[1])[: ref.shape[0]]

        for at, back in enumerate((back_a, back_b, back_c)):
            put(outs[2 * at], sum(back[2 * k + 1 : 2 * k + 2, :] for k in range(micro)))
            put(outs[2 * at + 1], sum(back[2 * k : 2 * k + 1, :] for k in range(micro)))
        put(outs[6], back_a[2 * micro : 2 * micro + 1, :c_mid])
        put(outs[7], back_a[2 * micro + 1 : 2 * micro + 2, :c_mid])
        firsts = [first_rows(sums_a, k, c_in) for k in range(micro)]
        stats = [[f[0] for f in firsts]]
        for sums in (sums_b, sums_c):
            stats.append(
                [finish_rows(sums[2 * k : 2 * k + 2, :], firsts[k][2]) for k in range(micro)]
            )
        for at, history in enumerate(stats):
            for part in range(2):
                lanes = history[0][part].shape[1]
                value = running[2 * at + part][...]
                if value.shape[0] < lanes:
                    value = jnp.pad(value, (0, lanes - value.shape[0]))
                value = value.reshape(1, lanes)
                for k in range(micro):
                    value = (1.0 - MOMENTUM) * value + MOMENTUM * history[k][part]
                put(outs[8 + 2 * at + part], value)

    widths = [c_in] * 2 + [c_mid] * 2 + [c_res] * 2
    shapes = widths + [c_mid, c_mid] + widths
    tables = [(8, c_lane), (8, c_mid), (8, c_res)] * 2
    return call(
        "small_outputs",
        body,
        (1,),
        [whole(s) for s in tables] + [whole((n,)) for n in widths],
        [whole((n,)) for n in shapes],
        [shape_of((n,)) for n in shapes],
    )


def partner(array):
    return lax.ppermute(array, "section", [(0, 1), (1, 0)])


def share(rows):
    devices = lax.axis_size("section") * lax.axis_size("dp")
    bits = [1 << at for at in range(devices.bit_length() - 1)]
    groups = [[bits[-1], bits[0]]]
    rest = bits[1:-1]
    while rest:
        groups.append(rest[:2])
        rest = rest[2:]
    for group in groups:
        masks = [0]
        for bit in group:
            masks += [mask + bit for mask in masks]
        parts = [
            lax.ppermute(rows, BOTH, [(i, i ^ mask) for i in range(devices)]) if mask else rows
            for mask in masks
        ]
        while len(parts) > 1:
            parts = [a + b for a, b in zip(parts[::2], parts[1::2])]
        rows = parts[0]
    return rows


def shards(
    features,
    lengths,
    gain_first,
    shift_first,
    conv_first,
    bias_first,
    gain_second,
    shift_second,
    conv_second,
    gain_third,
    shift_third,
    conv_point,
    bias_point,
    mean_first,
    variance_first,
    mean_second,
    variance_second,
    mean_third,
    variance_third,
    cotangent,
):
    micro, _, bins, c_in = features.shape
    pooled = bins // 2
    taps, _, c_mid = conv_first.shape
    taps_b, _, c_res = conv_second.shape
    c_lane = up(c_in, LANES)
    section = lax.axis_index("section").astype(jnp.int32)
    lead = section == 0
    own_lengths = jnp.where(lead, lengths[:, 0], lengths[:, 1]).astype(jnp.int32)
    info = jnp.concatenate([section[None], own_lengths])
    feats = features.transpose(0, 3, 1, 2)

    loaded, part = load_features(micro, bins, c_in)(info, feats)
    sums_a = share(part)
    vectors = (
        gain_first, shift_first, bias_first, gain_second, shift_second, gain_third, shift_third,
        bias_point,
    )
    table = prepare_table(vectors, c_lane)(info, *vectors)
    act_a = activate(micro, c_in, taps, pooled)(info, loaded, sums_a, table)
    hid, diff, part = forward_first(micro, c_in, c_mid, taps, pooled)(info, act_a, table, conv_first)
    sums_b = share(part)
    go, up_c, grad_bias = turn_cotangent(micro, c_mid, c_res, pooled)(info, cotangent, conv_point)
    conv_b, act_b, part = forward_second(micro, c_in, c_mid, c_res, taps_b, pooled, c_lane)(
        info, hid, sums_a, sums_b, table, conv_second, grad_bias
    )
    sums_c = share(part)
    act_c, d_c, part = norm_third(micro, c_in, c_res, pooled, c_lane)(
        info, conv_b, up_c, sums_a, sums_c, table
    )
    back_c = share(part)
    d_b, part, stack_b = backward_second(micro, c_in, c_mid, c_res, taps_b, pooled, c_lane)(
        info, d_c, conv_b, sums_a, sums_b, sums_c, back_c, table, hid, conv_second
    )
    back_b = share(part)
    grad_second, grad_point = weights_second(micro, c_mid, c_res, taps_b, pooled)(
        info, act_b, stack_b, go, act_c
    )
    g_a, bias_sum = gradient_first(micro, c_in, c_mid, taps, pooled, c_lane)(
        info, d_b, hid, go, diff, sums_a, sums_b, back_b, table, grad_second
    )
    grad_first = weights_first(micro, c_in, c_mid, taps, pooled)(
        info, act_a, g_a, g_a, bias_sum
    )
    sums = lax.psum((grad_first, grad_second, grad_point), BOTH)
    running = (
        mean_first, variance_first, mean_second, variance_second, mean_third, variance_third,
    )

    def behind(_):
        d_a, part = backward_first(micro, c_in, c_mid, taps, pooled, c_lane)(
            info, g_a, loaded, sums_a, table, conv_first, bias_sum, grad_bias
        )
        back_a = share(part)
        own_out, send_out = point_output(micro, c_mid, c_res, pooled, c_lane)(
            info, act_c, hid, table, conv_point
        )
        got_out = partner(send_out)
        own_in, send_in = finish_first(micro, c_in, pooled, c_lane)(
            info, d_a, loaded, sums_a, back_a, table
        )
        got_in = partner(send_in)
        small = small_outputs(micro, c_in, c_mid, c_res, c_lane)(
            info, sums_a, sums_b, sums_c, back_a, back_b, back_c, *running
        )
        paired = pair_windows(micro, c_in // 2, bins)(info, own_in, got_in)
        block_output = jnp.stack(
            [jnp.where(lead, own_out, got_out), jnp.where(lead, got_out, own_out)], axis=1
        )
        return paired, block_output, tuple(small)

    def nothing(_):
        shapes = jax.eval_shape(behind, 0)
        return jax.tree.map(lambda s: jnp.zeros(s.shape, s.dtype), shapes)

    paired, block_output, small = lax.cond(info[1] > 0, behind, nothing, 0)
    input_grad = paired.transpose(0, 2, 3, 1)
    sum_first, sum_second, sum_point = widen(*(value.shape for value in sums))(info, *sums)
    return (
        block_output,
        input_grad,
        small[0],
        small[1],
        sum_first,
        small[6],
        small[2],
        small[3],
        sum_second,
        small[4],
        small[5],
        sum_point,
        small[7],
        *small[8:],
    )


def solution(mesh):
    wide_spec = P(None, "dp", None, None)
    split_spec = P(None, "dp", None, "section")
    return jax.shard_map(
        shards,
        mesh=mesh,
        in_specs=(wide_spec, P(None, "dp")) + (P(),) * 17 + (wide_spec,),
        out_specs=(split_spec, split_spec) + (P(),) * 17,
        check_vma=False,
    )
```
